256 devices in a mesh: sec: 16 (over y, x), mpo: 16 (over z, core).
Axes of the slice: x: 4, y: 4, z: 8, core: 2. Of those that a mesh axis runs over, the one named last changes fastest.
Arguments:
- wavefunction: bfloat16 [256, 128, 128], P('sec')
- left_size: int32 [256], P('sec'), may hold values from 32 to 128, as said below
- right_size: int32 [256], replicated, may hold values from 32 to 128, as said below
- right_sector: int32 [256], replicated, may hold values from 0 to 255, as said below
- left_environment: bfloat16 [32, 256, 128, 128], P('mpo', 'sec')
- right_environment: bfloat16 [32, 256, 128, 128], P('mpo', 'sec')
- term_weights: float32 [32], P('mpo'), may hold values from -0.4 to 0.4
Outputs:
- next_vector: float32 [256, 128, 128], P('sec', 'mpo')
- residual: float32 [256, 128, 128], P('sec', 'mpo')
- coefficients: float32 [3], replicated
The draws below stay inside these ranges and needn't reach their ends.
Inputs may be any that keep to these rules, and one draw needn't show every extreme that they name: `left_size`: some left sector has all 128 rows live. `right_size`: some right sector has all 128 columns live. `right_sector`: a permutation of the 256 sectors; of the left sectors of one index of sec (16 in a row) at most 2 pair with right sectors of any one index of sec (also 16 in a row), and some such pair of indices has exactly 2.
All inputs are finite; a program needn't handle non-finite values.
Results may differ from the reference program's by a relative error of at most 0.0064.
Values may be sent and summed in bfloat16 or wider, within the bound.
No kernel may reach another device: no remote copies, remote signals or barrier semaphores. Data moves between devices by JAX's collectives and lax.ppermute only.
A program may use at most 64 MiB of HBM per device.

```python
import math
import jax
import jax.numpy as jnp
from jax import lax

B = 128
SEC_DEV = 16
NSEC = 256
WT = 32


def scaled_field(key_noise, key_rows, key_cols, log_top):
    base_values = jax.random.normal(key_noise, (NSEC, B, B), jnp.float32)
    row_scale = jnp.exp(jax.random.uniform(key_rows, (NSEC, B, 1), jnp.float32, 0.0, log_top))
    col_scale = jnp.exp(jax.random.uniform(key_cols, (NSEC, 1, B), jnp.float32, 0.0, log_top))
    rising = 1.0 + 2.0 * jnp.arange(NSEC, dtype=jnp.float32) / max(NSEC - 1, 1)
    return base_values * row_scale * col_scale * rising[:, None, None] / 10.0


def draw_wavefunction(key, part):
    key = jax.random.fold_in(key, 11)
    key_noise, key_rows, key_cols = jax.random.split(key, 3)
    return scaled_field(key_noise, key_rows, key_cols, 2.3).astype(jnp.bfloat16)


def sector_sizes(key):
    key_sizes, key_full = jax.random.split(key)
    drawn_size = jax.random.randint(key_sizes, (NSEC,), B // 4, B + 1)
    full_index = jax.random.randint(key_full, (), 0, NSEC)
    return jnp.where(jnp.arange(NSEC) == full_index, B, drawn_size).astype(jnp.int32)


def draw_left_size(key, part):
    key = jax.random.fold_in(key, 23)
    return sector_sizes(key)


def draw_right_size(key, part):
    key = jax.random.fold_in(key, 29)
    return sector_sizes(key)


def draw_right_sector(key, part):
    key = jax.random.fold_in(key, 41)
    key_spread, key_offset, key_shuffle, key_order = jax.random.split(key, 4)
    devices = NSEC // SEC_DEV
    average = SEC_DEV // devices
    surplus = max(1, average // 2)
    base_values = jnp.zeros((devices,), jnp.int32).at[0].set(surplus).at[1].set(-surplus)
    spread = jax.random.permutation(key_spread, base_values)
    offset = jax.random.randint(key_offset, (), 0, devices)
    source_ids = jnp.arange(devices, dtype=jnp.int32)[:, None]
    target_ids = jnp.arange(devices, dtype=jnp.int32)[None, :]
    counts = average + spread[(target_ids - source_ids + offset) % devices]
    limits = jnp.cumsum(counts, axis=1)
    slot_ids = jnp.arange(SEC_DEV, dtype=jnp.int32)
    dest_sorted = jnp.sum((limits[:, None, :] <= slot_ids[None, :, None]).astype(jnp.int32), axis=2)
    shuffles = jax.vmap(lambda one_key: jax.random.permutation(one_key, SEC_DEV))(jax.random.split(key_shuffle, devices))
    targets = jnp.take_along_axis(dest_sorted, shuffles, axis=1)
    flat_target = targets.reshape(-1)
    onehot = (flat_target[:, None] == jnp.arange(devices, dtype=jnp.int32)[None, :]).astype(jnp.int32)
    arrival = jnp.sum((jnp.cumsum(onehot, axis=0) - onehot) * onehot, axis=1)
    orders = jax.vmap(lambda one_key: jax.random.permutation(one_key, SEC_DEV))(jax.random.split(key_order, devices))
    return (flat_target * SEC_DEV + orders[flat_target, arrival]).astype(jnp.int32)


def environment(key):
    key_noise, key_diag = jax.random.split(key)
    raw_noise = jax.random.normal(key_noise, (WT, NSEC, B, B), jnp.float32)
    symmetric = (raw_noise + jnp.swapaxes(raw_noise, 2, 3)) * (1.0 / math.sqrt(2.0 * B))
    diag_shift = jax.random.uniform(key_diag, (WT, NSEC, 1, 1), jnp.float32, 0.5, 1.5)
    positions = jnp.arange(B, dtype=jnp.int32)
    identity = (positions[:, None] == positions[None, :]).astype(jnp.float32)
    return symmetric + diag_shift * identity[None, None, :, :]


def draw_left_environment(key, part):
    key = jax.random.fold_in(key, 53)
    return environment(key).astype(jnp.bfloat16)


def draw_right_environment(key, part):
    key = jax.random.fold_in(key, 59)
    return environment(key).astype(jnp.bfloat16)


def shard_levels(stream_key, dims, shards, least, high):
    factor_of = 1.0
    for position, parts in shards:
        draws = jax.random.uniform(jax.random.fold_in(jax.random.fold_in(stream_key, 6), position), (parts,), jnp.float32, least / len(shards), high / len(shards))
        factor_of = factor_of * jnp.repeat(jnp.exp(draws), dims[position] // parts).reshape((-1,) + (1,) * (len(dims) - 1 - position))
    return factor_of


def setup_inputs(seed: int = 0) -> dict:
    key_list = jax.random.split(jax.random.key(seed), 8)
    wavefunction = draw_wavefunction(jax.random.fold_in(key_list[7], 71), 0)
    left_size = draw_left_size(jax.random.fold_in(key_list[7], 71), 0)
    right_size = draw_right_size(jax.random.fold_in(key_list[7], 71), 0)
    right_sector = draw_right_sector(jax.random.fold_in(key_list[7], 71), 0)
    left_environment = draw_left_environment(jax.random.fold_in(key_list[7], 71), 0)
    right_environment = draw_right_environment(jax.random.fold_in(key_list[7], 71), 0)
    term_weights = jnp.clip(jax.random.uniform(key_list[6], (WT,), jnp.float32, -0.4, 0.4) * shard_levels(key_list[6], (WT,), ((0, 16),), -0.4, 0.0), -0.4, 0.4)
    return dict(wavefunction=wavefunction, left_size=left_size, right_size=right_size, right_sector=right_sector, left_environment=left_environment, right_environment=right_environment, term_weights=term_weights)


def live_blocks(left_size, right_size, right_sector):
    positions = jnp.arange(B, dtype=jnp.int32)
    partner_size = jnp.take(right_size, right_sector, axis=0)
    row_live = (positions[None, :] < left_size[:, None]).astype(jnp.float32)
    col_live = (positions[None, :] < partner_size[:, None]).astype(jnp.float32)
    return row_live[:, :, None] * col_live[:, None, :]

def apply_operator(vector, live_mask, left_environment, right_environment, right_sector, term_weights):
    rounded = vector.astype(jnp.bfloat16)

    def one_sector(inputs):
        sector_block, sector, partner = inputs
        left_terms = lax.dynamic_index_in_dim(left_environment, sector, 1, keepdims=False)
        right_terms = lax.dynamic_index_in_dim(right_environment, partner, 1, keepdims=False)
        half_term = jnp.einsum('wab,bc->wac', left_terms.astype(jnp.float32), sector_block.astype(jnp.float32))
        half_term = (term_weights[:, None, None] * half_term).astype(jnp.bfloat16)
        return jnp.einsum('wac,wdc->ad', half_term.astype(jnp.float32), right_terms.astype(jnp.float32))
    sectors = jnp.arange(NSEC, dtype=jnp.int32)
    applied = lax.map(one_sector, (rounded, sectors, right_sector.astype(jnp.int32)))
    return live_mask * applied

def reference(wavefunction, left_size, right_size, right_sector, left_environment, right_environment, term_weights):
    live_mask = live_blocks(left_size, right_size, right_sector)
    entries = float(NSEC * B * B)
    masked_start = live_mask * wavefunction.astype(jnp.float32)
    first_vector = masked_start / jnp.sqrt(jnp.sum(masked_start * masked_start) / entries + 1e-06)
    image_first = apply_operator(first_vector, live_mask, left_environment, right_environment, right_sector, term_weights)
    alpha_first = jnp.sum(first_vector * image_first) / entries
    lanczos_rest = image_first - alpha_first * first_vector
    beta_next = jnp.sqrt(jnp.sum(lanczos_rest * lanczos_rest) / entries + 1e-06)
    next_vector = lanczos_rest / beta_next
    image_next = apply_operator(next_vector, live_mask, left_environment, right_environment, right_sector, term_weights)
    alpha_next = jnp.sum(next_vector * image_next) / entries
    residual = image_next - alpha_next * next_vector - beta_next * first_vector
    coefficients = jnp.stack([alpha_first, beta_next, alpha_next])
    return (next_vector, residual, coefficients)
```

```python
import jax
import jax.numpy as jnp
from jax import lax
from jax.experimental import pallas as pl
from jax.experimental.pallas import tpu as pltpu
from jax.sharding import PartitionSpec as P

F32 = jnp.float32
BF16 = jnp.bfloat16
SLOTS = 2
PAD = 16
LANES = 8
MIB = 1024 * 1024


def pack_kernel(right_sector, weights, left_env, right_env, right_out, left_out, wbuf, sem):
    terms, blocks, width, _ = left_env.shape
    devices = right_out.shape[0]
    sec = lax.axis_index("sec")
    row = lax.broadcasted_iota(jnp.int32, wbuf.shape, 0)
    vals = jnp.zeros(wbuf.shape, F32)
    for w in range(terms):
        whole = jnp.full(wbuf.shape, weights[w], F32)
        high = whole.astype(BF16).astype(F32)
        mid = (whole - high).astype(BF16).astype(F32)
        low = whole - high - mid
        for j, part in enumerate((high, mid, low)):
            vals = jnp.where(row == w * 3 + j, part, vals)
    wbuf[...] = vals.astype(BF16)
    copies = []
    for q in range(blocks):
        for w in range(terms):
            copies.append(pltpu.make_async_copy(left_env.at[w, q], left_out.at[q, pl.ds(w * width, width)], sem.at[0]))
        copies.append(pltpu.make_async_copy(wbuf, left_out.at[q, pl.ds(terms * width, PAD)], sem.at[0]))
    for copy in copies:
        copy.start()
    for t in range(devices):
        first = jnp.int32(-1)
        last = jnp.int32(0)
        for i in range(blocks):
            sector = right_sector[t * blocks + i]
            match = sector // blocks == sec
            local = sector % blocks
            first = jnp.where(match & (first < 0), local, first)
            last = jnp.where(match, local, last)
        first = jnp.maximum(first, 0)
        for k, index in enumerate((first, last)):
            copy = pltpu.make_async_copy(right_env.at[:, index], right_out.at[t, k], sem.at[1])
            copy.start()
            copies.append(copy)
    for copy in copies:
        copy.wait()


def order_kernel(right_sector, arrived, ordered, sem):
    blocks = ordered.shape[0]
    sec = lax.axis_index("sec")
    sources = [right_sector[sec * blocks + q] // blocks for q in range(blocks)]
    copies = []
    for q in range(blocks):
        again = jnp.bool_(False)
        for other in range(q):
            again = again | (sources[other] == sources[q])
        copy = pltpu.make_async_copy(arrived.at[sources[q], jnp.where(again, 1, 0)], ordered.at[q], sem)
        copy.start()
        copies.append(copy)
    for copy in copies:
        copy.wait()


def live(rows, left, right):
    row = lax.broadcasted_iota(jnp.int32, rows, 0)
    col = lax.broadcasted_iota(jnp.int32, rows, 1)
    return (row < left) & (col < right)


def total(x):
    return jnp.sum(jnp.sum(x, axis=0, keepdims=True), axis=1, keepdims=True)


def lanczos_kernel(left_size, right_size, right_sector, vector, left_terms, right_terms, out):
    sources, _, width = left_terms.shape
    terms = right_terms.shape[1]
    sec = lax.axis_index("sec")
    own = lax.axis_index("mpo")
    blocks = left_size.shape[0]
    mask = live((width, width), left_size[own], right_size[right_sector[sec * blocks + own]])

    def apply(block):
        acc = jnp.zeros((width, width), F32)
        for p in range(sources):
            half = jnp.dot(left_terms[p, : terms * width], block, preferred_element_type=F32)
            scale = left_terms[p, terms * width :].astype(F32)
            for w in range(terms):
                weight = scale[3 * w : 3 * w + 1] + scale[3 * w + 1 : 3 * w + 2] + scale[3 * w + 2 : 3 * w + 3]
                term = (weight * half[w * width : (w + 1) * width]).astype(BF16)
                acc = acc + lax.dot_general(
                    term, right_terms[p, w], (((1,), (1,)), ((), ())), preferred_element_type=F32
                )
        return jnp.where(mask, acc, 0.0)

    start = jnp.where(mask, vector[0].astype(F32), 0.0)
    norm = total(start * start)
    scale = 1.0 / jnp.sqrt(norm / float(width * width) + 1e-06)
    image = apply(start.astype(BF16)) * scale
    unit = start * scale
    length = total(unit * unit)
    overlap = total(unit * image)
    ratio = jnp.where(length > 0.0, overlap / jnp.where(length > 0.0, length, 1.0), 0.0)
    rest = image - ratio * unit
    after = apply(rest.astype(BF16))
    numbers = (
        norm,
        overlap,
        ratio,
        total(rest * rest),
        total(rest * after),
        total(unit * after) + total(rest * image),
        total(rest * unit),
    )
    lane = lax.broadcasted_iota(jnp.int32, (8, width), 1)
    line = jnp.zeros((8, width), F32)
    for j, number in enumerate(numbers):
        line = jnp.where(lane == own * LANES + j, number, line)
    parts = out.shape[0]
    rows = width // parts
    for d in range(parts):
        out[d, :rows] = rest[d * rows : (d + 1) * rows]
        out[d, rows : 2 * rows] = after[d * rows : (d + 1) * rows]
        out[d, 2 * rows :] = line


def finish_kernel(left_size, right_size, right_sector, vector, pieces, shared, next_out, rest_out, coef_out):
    blocks, rows, width = vector.shape
    sec = lax.axis_index("sec")
    part = lax.axis_index("mpo")
    devices = shared.shape[0]
    entries = float(devices * blocks * width * width)
    cells = float(width * width)
    stats = shared[:, 0, :]
    lane = lax.broadcasted_iota(jnp.int32, stats.shape, 1) % LANES

    def field(x, j):
        return x if j == 0 else pltpu.roll(x, x.shape[1] - j, 1)

    lead = lane == 0
    norm = jnp.where(lead, field(stats, 0), 0.0)
    overlap = field(stats, 1)
    ratio = field(stats, 2)
    gain = 1.0 / jnp.sqrt(total(norm) / entries + 1e-06)
    mean = jnp.where(lead, norm, 0.0) / cells + 1e-06
    weight = jnp.where(lead, (gain * gain) * mean, 0.0)
    length = norm / mean
    alpha = total(jnp.where(lead, weight * overlap, 0.0)) / entries
    delta = jnp.where(lead, ratio - alpha, 0.0)
    rest_total = total(jnp.where(lead, weight * (field(stats, 3) + delta * delta * length + 2.0 * delta * field(stats, 6)), 0.0))
    beta = jnp.sqrt(rest_total / entries + 1e-06)
    inner = field(stats, 4) + delta * field(stats, 5) + delta * delta * overlap
    alpha_next = total(jnp.where(lead, weight * inner, 0.0)) / entries / beta / beta
    coef_lane = lax.broadcasted_iota(jnp.int32, coef_out.shape, 1)
    coef_out[...] = jnp.where(coef_lane == 0, alpha, jnp.where(coef_lane == 1, beta, alpha_next))
    for q in range(blocks):
        line = pieces[q, 2 * rows : 2 * rows + 1, :]
        lane_one = lax.broadcasted_iota(jnp.int32, line.shape, 1)
        norm_q = jnp.sum(jnp.where(lane_one == q * LANES, line, 0.0), axis=1, keepdims=True)
        ratio_q = jnp.sum(jnp.where(lane_one == q * LANES + 2, line, 0.0), axis=1, keepdims=True)
        root = jnp.sqrt(norm_q / cells + 1e-06)
        scale = gain * root
        row = lax.broadcasted_iota(jnp.int32, (rows, width), 0) + part * rows
        col = lax.broadcasted_iota(jnp.int32, (rows, width), 1)
        mask = (row < left_size[q]) & (col < right_size[right_sector[sec * blocks + q]])
        unit = jnp.where(mask, vector[q].astype(F32), 0.0) / root
        rest = pieces[q, :rows]
        after = pieces[q, rows : 2 * rows]
        shift = ratio_q - alpha
        second = (scale / beta) * (rest + shift * unit)
        image = (scale / beta) * (after + shift * (rest + ratio_q * unit))
        next_out[q] = second
        rest_out[q] = image - alpha_next * second - (beta * scale) * unit


def shards(
    wavefunction,
    left_size,
    right_size,
    right_sector,
    left_environment,
    right_environment,
    term_weights,
):
    blocks, width, _ = wavefunction.shape
    terms = left_environment.shape[0]
    devices = lax.axis_size("sec")
    layers = lax.axis_size("mpo")
    rows = width // layers
    own = lax.axis_index("mpo")
    anywhere = pl.BlockSpec(memory_space=pl.ANY)
    scalars = pl.BlockSpec(memory_space=pltpu.SMEM)
    vmem = pl.BlockSpec(memory_space=pltpu.VMEM)

    with jax.named_scope("pack"):
        right_out, left_out = pl.pallas_call(
            pack_kernel,
            out_shape=(
                jax.ShapeDtypeStruct((devices, SLOTS, terms, width, width), BF16),
                jax.ShapeDtypeStruct((blocks, terms * width + PAD, width), BF16),
            ),
            in_specs=[scalars, scalars, anywhere, anywhere],
            out_specs=(anywhere, anywhere),
            scratch_shapes=[pltpu.VMEM((PAD, width), BF16), pltpu.SemaphoreType.DMA((2,))],
            compiler_params=pltpu.CompilerParams(vmem_limit_bytes=4 * MIB),
        )(right_sector, term_weights, left_environment, right_environment)
    with jax.named_scope("right_over_sec"):
        arrived = lax.all_to_all(right_out, "sec", 0, 0, tiled=True)
    with jax.named_scope("left_over_mpo"):
        left_terms = lax.all_to_all(left_out, "mpo", 0, 0, tiled=True)
    with jax.named_scope("order"):
        ordered = pl.pallas_call(
            order_kernel,
            out_shape=jax.ShapeDtypeStruct((blocks, terms, width, width), BF16),
            in_specs=[scalars, anywhere],
            out_specs=anywhere,
            scratch_shapes=[pltpu.SemaphoreType.DMA],
            compiler_params=pltpu.CompilerParams(vmem_limit_bytes=4 * MIB),
        )(right_sector, arrived)
    with jax.named_scope("right_over_mpo"):
        right_terms = lax.all_to_all(ordered, "mpo", 0, 0, tiled=True)
    with jax.named_scope("lanczos"):
        vector = lax.dynamic_slice_in_dim(wavefunction, own, 1, 0)
        pieces = pl.pallas_call(
            lanczos_kernel,
            out_shape=jax.ShapeDtypeStruct((layers, 2 * rows + 8, width), F32),
            in_specs=[scalars, scalars, scalars, vmem, vmem, vmem],
            out_specs=vmem,
            compiler_params=pltpu.CompilerParams(vmem_limit_bytes=16 * MIB),
        )(left_size, right_size, right_sector, vector, left_terms, right_terms)
    with jax.named_scope("rows_over_mpo"):
        pieces = lax.all_to_all(pieces, "mpo", 0, 0, tiled=True)
    with jax.named_scope("numbers_over_sec"):
        line = jnp.sum(pieces[:, 2 * rows :, :], axis=0)
        shared = lax.all_to_all(jnp.broadcast_to(line[None], (devices, 8, width)), "sec", 0, 0, tiled=True)
    with jax.named_scope("finish"):
        own_rows = lax.dynamic_slice_in_dim(wavefunction, own * rows, rows, 1)
        next_vector, residual, coefficients = pl.pallas_call(
            finish_kernel,
            out_shape=(
                jax.ShapeDtypeStruct((blocks, rows, width), F32),
                jax.ShapeDtypeStruct((blocks, rows, width), F32),
                jax.ShapeDtypeStruct((1, width), F32),
            ),
            in_specs=[scalars, scalars, scalars, vmem, vmem, vmem],
            out_specs=(vmem, vmem, vmem),
            compiler_params=pltpu.CompilerParams(vmem_limit_bytes=8 * MIB),
        )(left_size, right_size, right_sector, own_rows, pieces, shared)
    return (next_vector, residual, coefficients[0, :3])


def solution(mesh):
    placed = (
        P("sec", None, None),
        P("sec"),
        P(),
        P(),
        P("mpo", "sec", None, None),
        P("mpo", "sec", None, None),
        P("mpo"),
    )
    return jax.shard_map(
        shards,
        mesh=mesh,
        in_specs=placed,
        out_specs=(P("sec", "mpo", None), P("sec", "mpo", None), P()),
        check_vma=False,
    )
```

```python
import jax
import jax.numpy as jnp
from jax import lax
from jax.experimental import pallas as pl
from jax.experimental.pallas import tpu as pltpu
from jax.sharding import PartitionSpec as P

F32 = jnp.float32
BF16 = jnp.bfloat16
SLOTS = 2
PAD = 16
LANES = 8
MIB = 1024 * 1024


def pack_right_kernel(right_sector, right_env, right_out, stage, sem):
    blocks = right_env.shape[1]
    devices = right_out.shape[0]
    sec = lax.axis_index("sec")
    load = pltpu.make_async_copy(right_env, stage, sem.at[0])
    load.start()
    picks = []
    for t in range(devices):
        first = jnp.int32(-1)
        last = jnp.int32(0)
        for i in range(blocks):
            sector = right_sector[t * blocks + i]
            match = sector // blocks == sec
            local = sector % blocks
            first = jnp.where(match & (first < 0), local, first)
            last = jnp.where(match, local, last)
        picks.append((jnp.maximum(first, 0), last))
    load.wait()
    copies = []
    for t in range(devices):
        for k in range(SLOTS):
            copies.append(pltpu.make_async_copy(stage.at[:, picks[t][k]], right_out.at[t, k], sem.at[1]))
            copies[-1].start()
    for copy in copies:
        copy.wait()


def pack_left_kernel(weights, left_env, kept, given, stage, wbuf, sem):
    terms, _, width, _ = left_env.shape
    chips = kept.shape[0]
    own = lax.axis_index("mpo")
    load = pltpu.make_async_copy(left_env, stage, sem.at[0])
    load.start()
    row = lax.broadcasted_iota(jnp.int32, wbuf.shape, 0)
    vals = jnp.zeros(wbuf.shape, F32)
    for w in range(terms):
        whole = jnp.full(wbuf.shape, weights[w], F32)
        high = whole.astype(BF16).astype(F32)
        mid = (whole - high).astype(BF16).astype(F32)
        low = whole - high - mid
        for j, part in enumerate((high, mid, low)):
            vals = jnp.where(row == w * 3 + j, part, vals)
    wbuf[...] = vals.astype(BF16)
    load.wait()
    copies = []
    for d in range(chips):
        chip = (own // 2 + d) % chips
        for target, core in ((kept, own % 2), (given, 1 - own % 2)):
            q = 2 * chip + core
            for w in range(terms):
                copies.append(pltpu.make_async_copy(stage.at[w, q], target.at[d, pl.ds(w * width, width)], sem.at[1]))
            copies.append(pltpu.make_async_copy(wbuf, target.at[d, pl.ds(terms * width, PAD)], sem.at[1]))
    for copy in copies:
        copy.start()
    for copy in copies:
        copy.wait()


def pair_kernel(kept, taken, *rest):
    *pairs, sem = rest
    copies = []
    for d, pair in enumerate(pairs):
        for half, source in enumerate((kept, taken)):
            copies.append(pltpu.make_async_copy(source.at[d], pair.at[half], sem))
            copies[-1].start()
    for copy in copies:
        copy.wait()


def order_kernel(right_sector, arrived, *rest):
    *_, ordered, sem = rest
    blocks = ordered.shape[0]
    sec = lax.axis_index("sec")
    sources = [right_sector[sec * blocks + q] // blocks for q in range(blocks)]
    copies = []
    for q in range(blocks):
        again = jnp.bool_(False)
        for other in range(q):
            again = again | (sources[other] == sources[q])
        copy = pltpu.make_async_copy(arrived.at[sources[q], jnp.where(again, 1, 0)], ordered.at[q], sem)
        copy.start()
        copies.append(copy)
    for copy in copies:
        copy.wait()


def live(rows, left, right):
    row = lax.broadcasted_iota(jnp.int32, rows, 0)
    col = lax.broadcasted_iota(jnp.int32, rows, 1)
    return (row < left) & (col < right)


def total(x):
    return jnp.sum(jnp.sum(x, axis=0, keepdims=True), axis=1, keepdims=True)


def lanczos_kernel(left_size, right_size, right_sector, vector, right_terms, *rest):
    *left_terms, out = rest
    sources, terms, width, _ = right_terms.shape
    chips = len(left_terms)
    sec = lax.axis_index("sec")
    own = lax.axis_index("mpo")
    blocks = left_size.shape[0]
    mask = live((width, width), left_size[own], right_size[right_sector[sec * blocks + own]])

    def apply(block):
        acc = jnp.zeros((width, width), F32)
        for move in range(sources):
            step, side = move // 2, move % 2
            source = 2 * ((own // 2 + chips - step) % chips) + (own % 2 + side) % 2
            half = jnp.dot(left_terms[step][side, : terms * width], block, preferred_element_type=F32)
            scale = left_terms[step][side, terms * width :].astype(F32)
            for w in range(terms):
                weight = scale[3 * w : 3 * w + 1] + scale[3 * w + 1 : 3 * w + 2] + scale[3 * w + 2 : 3 * w + 3]
                term = (weight * half[w * width : (w + 1) * width]).astype(BF16)
                acc = acc + lax.dot_general(
                    term, right_terms[source, w], (((1,), (1,)), ((), ())), preferred_element_type=F32
                )
        return jnp.where(mask, acc, 0.0)

    start = jnp.where(mask, vector[0].astype(F32), 0.0)
    norm = total(start * start)
    scale = 1.0 / jnp.sqrt(norm / float(width * width) + 1e-06)
    image = apply(start.astype(BF16)) * scale
    unit = start * scale
    length = total(unit * unit)
    overlap = total(unit * image)
    ratio = jnp.where(length > 0.0, overlap / jnp.where(length > 0.0, length, 1.0), 0.0)
    rest = image - ratio * unit
    after = apply(rest.astype(BF16))
    numbers = (
        norm,
        overlap,
        ratio,
        total(rest * rest),
        total(rest * after),
        total(unit * after) + total(rest * image),
        total(rest * unit),
    )
    lane = lax.broadcasted_iota(jnp.int32, (8, width), 1)
    line = jnp.zeros((8, width), F32)
    for j, number in enumerate(numbers):
        line = jnp.where(lane == own * LANES + j, number, line)
    parts = out.shape[0]
    rows = width // parts
    for d in range(parts):
        out[d, :rows] = rest[d * rows : (d + 1) * rows]
        out[d, rows : 2 * rows] = after[d * rows : (d + 1) * rows]
        out[d, 2 * rows :] = line


def finish_kernel(left_size, right_size, right_sector, vector, pieces, shared, next_out, rest_out, coef_out):
    blocks, rows, width = vector.shape
    sec = lax.axis_index("sec")
    part = lax.axis_index("mpo")
    devices = shared.shape[0]
    entries = float(devices * blocks * width * width)
    cells = float(width * width)
    stats = shared[:, 0, :]
    lane = lax.broadcasted_iota(jnp.int32, stats.shape, 1) % LANES

    def field(x, j):
        return x if j == 0 else pltpu.roll(x, x.shape[1] - j, 1)

    lead = lane == 0
    norm = jnp.where(lead, field(stats, 0), 0.0)
    overlap = field(stats, 1)
    ratio = field(stats, 2)
    gain = 1.0 / jnp.sqrt(total(norm) / entries + 1e-06)
    mean = jnp.where(lead, norm, 0.0) / cells + 1e-06
    weight = jnp.where(lead, (gain * gain) * mean, 0.0)
    length = norm / mean
    alpha = total(jnp.where(lead, weight * overlap, 0.0)) / entries
    delta = jnp.where(lead, ratio - alpha, 0.0)
    rest_total = total(jnp.where(lead, weight * (field(stats, 3) + delta * delta * length + 2.0 * delta * field(stats, 6)), 0.0))
    beta = jnp.sqrt(rest_total / entries + 1e-06)
    inner = field(stats, 4) + delta * field(stats, 5) + delta * delta * overlap
    alpha_next = total(jnp.where(lead, weight * inner, 0.0)) / entries / beta / beta
    coef_lane = lax.broadcasted_iota(jnp.int32, coef_out.shape, 1)
    coef_out[...] = jnp.where(coef_lane == 0, alpha, jnp.where(coef_lane == 1, beta, alpha_next))
    for q in range(blocks):
        line = pieces[q, 2 * rows : 2 * rows + 1, :]
        lane_one = lax.broadcasted_iota(jnp.int32, line.shape, 1)
        norm_q = jnp.sum(jnp.where(lane_one == q * LANES, line, 0.0), axis=1, keepdims=True)
        ratio_q = jnp.sum(jnp.where(lane_one == q * LANES + 2, line, 0.0), axis=1, keepdims=True)
        root = jnp.sqrt(norm_q / cells + 1e-06)
        scale = gain * root
        row = lax.broadcasted_iota(jnp.int32, (rows, width), 0) + part * rows
        col = lax.broadcasted_iota(jnp.int32, (rows, width), 1)
        mask = (row < left_size[q]) & (col < right_size[right_sector[sec * blocks + q]])
        unit = jnp.where(mask, vector[q].astype(F32), 0.0) / root
        rest = pieces[q, :rows]
        after = pieces[q, rows : 2 * rows]
        shift = ratio_q - alpha
        second = (scale / beta) * (rest + shift * unit)
        image = (scale / beta) * (after + shift * (rest + ratio_q * unit))
        next_out[q] = second
        rest_out[q] = image - alpha_next * second - (beta * scale) * unit


def shards(
    wavefunction,
    left_size,
    right_size,
    right_sector,
    left_environment,
    right_environment,
    term_weights,
):
    blocks, width, _ = wavefunction.shape
    terms = left_environment.shape[0]
    devices = lax.axis_size("sec")
    layers = lax.axis_size("mpo")
    rows = width // layers
    own = lax.axis_index("mpo")
    anywhere = pl.BlockSpec(memory_space=pl.ANY)
    scalars = pl.BlockSpec(memory_space=pltpu.SMEM)
    vmem = pl.BlockSpec(memory_space=pltpu.VMEM)

    chips = layers // 2
    long = terms * width + PAD
    with jax.named_scope("pack_right"):
        right_out = pl.pallas_call(
            pack_right_kernel,
            out_shape=jax.ShapeDtypeStruct((devices, SLOTS, terms, width, width), BF16),
            in_specs=[scalars, anywhere],
            out_specs=anywhere,
            scratch_shapes=[pltpu.VMEM(right_environment.shape, BF16), pltpu.SemaphoreType.DMA((2,))],
            compiler_params=pltpu.CompilerParams(vmem_limit_bytes=60 * MIB),
        )(right_sector, right_environment)
    with jax.named_scope("right_over_sec"):
        arrived = lax.all_to_all(right_out, "sec", 0, 0, tiled=True)
    with jax.named_scope("pack_left"):
        kept, given = pl.pallas_call(
            pack_left_kernel,
            out_shape=(jax.ShapeDtypeStruct((chips, long, width), BF16),) * 2,
            in_specs=[scalars, anywhere],
            out_specs=(anywhere, anywhere),
            scratch_shapes=[
                pltpu.VMEM(left_environment.shape, BF16),
                pltpu.VMEM((PAD, width), BF16),
                pltpu.SemaphoreType.DMA((2,)),
            ],
            compiler_params=pltpu.CompilerParams(vmem_limit_bytes=8 * MIB),
        )(term_weights, left_environment)
    with jax.named_scope("left_over_core"):
        taken = lax.ppermute(given, "mpo", [(p, p ^ 1) for p in range(layers)])
    with jax.named_scope("pair"):
        pairs = pl.pallas_call(
            pair_kernel,
            out_shape=(jax.ShapeDtypeStruct((2, long, width), BF16),) * chips,
            in_specs=[anywhere, anywhere],
            out_specs=(anywhere,) * chips,
            scratch_shapes=[pltpu.SemaphoreType.DMA],
            compiler_params=pltpu.CompilerParams(vmem_limit_bytes=4 * MIB),
        )(kept, taken)
    with jax.named_scope("left_over_z"):
        left_terms = list(pairs)
        for d in sorted(range(1, chips), key=lambda d: -min(d, chips - d)):
            route = [(p, (p + 2 * d) % layers) for p in range(layers)]
            left_terms[d] = lax.ppermute(pairs[d], "mpo", route)
    with jax.named_scope("order"):
        ordered = pl.pallas_call(
            order_kernel,
            out_shape=jax.ShapeDtypeStruct((blocks, terms, width, width), BF16),
            in_specs=[scalars] + [anywhere] * chips,
            out_specs=anywhere,
            scratch_shapes=[pltpu.SemaphoreType.DMA],
            compiler_params=pltpu.CompilerParams(vmem_limit_bytes=4 * MIB),
        )(right_sector, arrived, *left_terms[1:])
    with jax.named_scope("right_over_mpo"):
        right_terms = lax.all_to_all(ordered, "mpo", 0, 0, tiled=True)
    with jax.named_scope("lanczos"):
        vector = lax.dynamic_slice_in_dim(wavefunction, own, 1, 0)
        pieces = pl.pallas_call(
            lanczos_kernel,
            out_shape=jax.ShapeDtypeStruct((layers, 2 * rows + 8, width), F32),
            in_specs=[scalars, scalars, scalars, vmem, vmem] + [vmem] * chips,
            out_specs=vmem,
            compiler_params=pltpu.CompilerParams(vmem_limit_bytes=16 * MIB),
        )(left_size, right_size, right_sector, vector, right_terms, *left_terms)
    with jax.named_scope("rows_over_mpo"):
        pieces = lax.all_to_all(pieces, "mpo", 0, 0, tiled=True)
    with jax.named_scope("numbers_over_sec"):
        line = jnp.sum(pieces[:, 2 * rows :, :], axis=0)
        shared = lax.all_to_all(jnp.broadcast_to(line[None], (devices, 8, width)), "sec", 0, 0, tiled=True)
    with jax.named_scope("finish"):
        own_rows = lax.dynamic_slice_in_dim(wavefunction, own * rows, rows, 1)
        next_vector, residual, coefficients = pl.pallas_call(
            finish_kernel,
            out_shape=(
                jax.ShapeDtypeStruct((blocks, rows, width), F32),
                jax.ShapeDtypeStruct((blocks, rows, width), F32),
                jax.ShapeDtypeStruct((1, width), F32),
            ),
            in_specs=[scalars, scalars, scalars, vmem, vmem, vmem],
            out_specs=(vmem, vmem, vmem),
            compiler_params=pltpu.CompilerParams(vmem_limit_bytes=8 * MIB),
        )(left_size, right_size, right_sector, own_rows, pieces, shared)
    return (next_vector, residual, coefficients[0, :3])


def solution(mesh):
    placed = (
        P("sec", None, None),
        P("sec"),
        P(),
        P(),
        P("mpo", "sec", None, None),
        P("mpo", "sec", None, None),
        P("mpo"),
    )
    return jax.shard_map(
        shards,
        mesh=mesh,
        in_specs=placed,
        out_specs=(P("sec", "mpo", None), P("sec", "mpo", None), P()),
        check_vma=False,
    )
```

```python
import jax
import jax.numpy as jnp
from jax import lax
from jax.experimental import pallas as pl
from jax.experimental.pallas import tpu as pltpu
from jax.sharding import PartitionSpec as P

F32 = jnp.float32
BF16 = jnp.bfloat16
SLOTS = 2
PAD = 16
LANES = 8
MIB = 1024 * 1024


def pack_right_kernel(right_sector, right_env, right_out, stage, sem):
    blocks = right_env.shape[1]
    devices = right_out.shape[0]
    sec = lax.axis_index("sec")
    load = pltpu.make_async_copy(right_env, stage, sem.at[0])
    load.start()
    picks = []
    for t in range(devices):
        first = jnp.int32(-1)
        last = jnp.int32(0)
        for i in range(blocks):
            sector = right_sector[t * blocks + i]
            match = sector // blocks == sec
            local = sector % blocks
            first = jnp.where(match & (first < 0), local, first)
            last = jnp.where(match, local, last)
        picks.append((jnp.maximum(first, 0), last))
    load.wait()
    copies = []
    for t in range(devices):
        for k in range(SLOTS):
            copies.append(pltpu.make_async_copy(stage.at[:, picks[t][k]], right_out.at[t, k], sem.at[1]))
            copies[-1].start()
    for copy in copies:
        copy.wait()


def pack_left_kernel(weights, left_env, *rest):
    *pairs, stage, wbuf, sem = rest
    terms, _, width, _ = left_env.shape
    chips = len(pairs)
    own = lax.axis_index("mpo")
    load = pltpu.make_async_copy(left_env, stage, sem.at[0])
    load.start()
    row = lax.broadcasted_iota(jnp.int32, wbuf.shape, 0)
    vals = jnp.zeros(wbuf.shape, F32)
    for w in range(terms):
        whole = jnp.full(wbuf.shape, weights[w], F32)
        high = whole.astype(BF16).astype(F32)
        mid = (whole - high).astype(BF16).astype(F32)
        low = whole - high - mid
        for j, part in enumerate((high, mid, low)):
            vals = jnp.where(row == w * 3 + j, part, vals)
    wbuf[...] = vals.astype(BF16)
    load.wait()
    copies = []
    for d, pair in enumerate(pairs):
        chip = (own // 2 + d) % chips
        for side in range(2):
            q = 2 * chip + (own % 2 + side) % 2
            for w in range(terms):
                copies.append(pltpu.make_async_copy(stage.at[w, q], pair.at[side, pl.ds(w * width, width)], sem.at[1]))
            copies.append(pltpu.make_async_copy(wbuf, pair.at[side, pl.ds(terms * width, PAD)], sem.at[1]))
    for copy in copies:
        copy.start()
    for copy in copies:
        copy.wait()


def collect_kernel(*refs):
    *pairs, given, sem = refs
    copies = []
    for d, pair in enumerate(pairs):
        copies.append(pltpu.make_async_copy(pair.at[1], given.at[d], sem))
        copies[-1].start()
    for copy in copies:
        copy.wait()


def order_kernel(right_sector, arrived, ordered, stage, sem):
    blocks = ordered.shape[0]
    sec = lax.axis_index("sec")
    sources = [right_sector[sec * blocks + q] // blocks for q in range(blocks)]
    loads = []
    for q in range(blocks):
        again = jnp.bool_(False)
        for other in range(q):
            again = again | (sources[other] == sources[q])
        load = pltpu.make_async_copy(arrived.at[sources[q], jnp.where(again, 1, 0)], stage.at[q], sem.at[q])
        load.start()
        loads.append(load)
    stores = []
    for q in range(blocks):
        loads[q].wait()
        stores.append(pltpu.make_async_copy(stage.at[q], ordered.at[q], sem.at[blocks]))
        stores[-1].start()
    for store in stores:
        store.wait()


def live(rows, left, right):
    row = lax.broadcasted_iota(jnp.int32, rows, 0)
    col = lax.broadcasted_iota(jnp.int32, rows, 1)
    return (row < left) & (col < right)


def total(x):
    return jnp.sum(jnp.sum(x, axis=0, keepdims=True), axis=1, keepdims=True)


def lanczos_kernel(left_size, right_size, right_sector, vector, right_terms, taken, *rest):
    *left_terms, out = rest
    sources, terms, width, _ = right_terms.shape
    chips = len(left_terms)
    sec = lax.axis_index("sec")
    own = lax.axis_index("mpo")
    blocks = left_size.shape[0]
    mask = live((width, width), left_size[own], right_size[right_sector[sec * blocks + own]])

    def apply(block):
        acc = jnp.zeros((width, width), F32)
        for move in range(sources):
            step, side = move // 2, move % 2
            source = 2 * ((own // 2 + chips - step) % chips) + (own % 2 + side) % 2
            part = left_terms[step].at[0] if side == 0 else taken.at[step]
            half = jnp.dot(part[: terms * width], block, preferred_element_type=F32)
            scale = part[terms * width :].astype(F32)
            for w in range(terms):
                weight = scale[3 * w : 3 * w + 1] + scale[3 * w + 1 : 3 * w + 2] + scale[3 * w + 2 : 3 * w + 3]
                term = (weight * half[w * width : (w + 1) * width]).astype(BF16)
                acc = acc + lax.dot_general(
                    term, right_terms[source, w], (((1,), (1,)), ((), ())), preferred_element_type=F32
                )
        return jnp.where(mask, acc, 0.0)

    start = jnp.where(mask, vector[0].astype(F32), 0.0)
    norm = total(start * start)
    scale = 1.0 / jnp.sqrt(norm / float(width * width) + 1e-06)
    image = apply(start.astype(BF16)) * scale
    unit = start * scale
    length = total(unit * unit)
    overlap = total(unit * image)
    ratio = jnp.where(length > 0.0, overlap / jnp.where(length > 0.0, length, 1.0), 0.0)
    rest = image - ratio * unit
    after = apply(rest.astype(BF16))
    numbers = (
        norm,
        overlap,
        ratio,
        total(rest * rest),
        total(rest * after),
        total(unit * after) + total(rest * image),
        total(rest * unit),
    )
    lane = lax.broadcasted_iota(jnp.int32, (8, width), 1)
    line = jnp.zeros((8, width), F32)
    for j, number in enumerate(numbers):
        line = jnp.where(lane == own * LANES + j, number, line)
    parts = out.shape[0]
    rows = width // parts
    for d in range(parts):
        out[d, :rows] = rest[d * rows : (d + 1) * rows]
        out[d, rows : 2 * rows] = after[d * rows : (d + 1) * rows]
        out[d, 2 * rows :] = line


def finish_kernel(left_size, right_size, right_sector, vector, pieces, shared, next_out, rest_out, coef_out):
    blocks, rows, width = vector.shape
    sec = lax.axis_index("sec")
    part = lax.axis_index("mpo")
    devices = shared.shape[0]
    entries = float(devices * blocks * width * width)
    cells = float(width * width)
    stats = shared[:, 0, :]
    lane = lax.broadcasted_iota(jnp.int32, stats.shape, 1) % LANES

    def field(x, j):
        return x if j == 0 else pltpu.roll(x, x.shape[1] - j, 1)

    lead = lane == 0
    norm = jnp.where(lead, field(stats, 0), 0.0)
    overlap = field(stats, 1)
    ratio = field(stats, 2)
    gain = 1.0 / jnp.sqrt(total(norm) / entries + 1e-06)
    mean = jnp.where(lead, norm, 0.0) / cells + 1e-06
    weight = jnp.where(lead, (gain * gain) * mean, 0.0)
    length = norm / mean
    alpha = total(jnp.where(lead, weight * overlap, 0.0)) / entries
    delta = jnp.where(lead, ratio - alpha, 0.0)
    rest_total = total(jnp.where(lead, weight * (field(stats, 3) + delta * delta * length + 2.0 * delta * field(stats, 6)), 0.0))
    beta = jnp.sqrt(rest_total / entries + 1e-06)
    inner = field(stats, 4) + delta * field(stats, 5) + delta * delta * overlap
    alpha_next = total(jnp.where(lead, weight * inner, 0.0)) / entries / beta / beta
    coef_lane = lax.broadcasted_iota(jnp.int32, coef_out.shape, 1)
    coef_out[...] = jnp.where(coef_lane == 0, alpha, jnp.where(coef_lane == 1, beta, alpha_next))
    for q in range(blocks):
        line = pieces[q, 2 * rows : 2 * rows + 1, :]
        lane_one = lax.broadcasted_iota(jnp.int32, line.shape, 1)
        norm_q = jnp.sum(jnp.where(lane_one == q * LANES, line, 0.0), axis=1, keepdims=True)
        ratio_q = jnp.sum(jnp.where(lane_one == q * LANES + 2, line, 0.0), axis=1, keepdims=True)
        root = jnp.sqrt(norm_q / cells + 1e-06)
        scale = gain * root
        row = lax.broadcasted_iota(jnp.int32, (rows, width), 0) + part * rows
        col = lax.broadcasted_iota(jnp.int32, (rows, width), 1)
        mask = (row < left_size[q]) & (col < right_size[right_sector[sec * blocks + q]])
        unit = jnp.where(mask, vector[q].astype(F32), 0.0) / root
        rest = pieces[q, :rows]
        after = pieces[q, rows : 2 * rows]
        shift = ratio_q - alpha
        second = (scale / beta) * (rest + shift * unit)
        image = (scale / beta) * (after + shift * (rest + ratio_q * unit))
        next_out[q] = second
        rest_out[q] = image - alpha_next * second - (beta * scale) * unit


def shards(
    wavefunction,
    left_size,
    right_size,
    right_sector,
    left_environment,
    right_environment,
    term_weights,
):
    blocks, width, _ = wavefunction.shape
    terms = left_environment.shape[0]
    devices = lax.axis_size("sec")
    layers = lax.axis_size("mpo")
    rows = width // layers
    own = lax.axis_index("mpo")
    anywhere = pl.BlockSpec(memory_space=pl.ANY)
    scalars = pl.BlockSpec(memory_space=pltpu.SMEM)
    vmem = pl.BlockSpec(memory_space=pltpu.VMEM)

    chips = layers // 2
    long = terms * width + PAD
    with jax.named_scope("pack_right"):
        right_out = pl.pallas_call(
            pack_right_kernel,
            out_shape=jax.ShapeDtypeStruct((devices, SLOTS, terms, width, width), BF16),
            in_specs=[scalars, anywhere],
            out_specs=anywhere,
            scratch_shapes=[pltpu.VMEM(right_environment.shape, BF16), pltpu.SemaphoreType.DMA((2,))],
            compiler_params=pltpu.CompilerParams(vmem_limit_bytes=60 * MIB),
        )(right_sector, right_environment)
    with jax.named_scope("right_over_sec"):
        arrived = lax.all_to_all(right_out, "sec", 0, 0, tiled=True)
    with jax.named_scope("pack_left"):
        pairs = pl.pallas_call(
            pack_left_kernel,
            out_shape=(jax.ShapeDtypeStruct((2, long, width), BF16),) * chips,
            in_specs=[scalars, anywhere],
            out_specs=(anywhere,) * chips,
            scratch_shapes=[
                pltpu.VMEM(left_environment.shape, BF16),
                pltpu.VMEM((PAD, width), BF16),
                pltpu.SemaphoreType.DMA((2,)),
            ],
            compiler_params=pltpu.CompilerParams(vmem_limit_bytes=8 * MIB),
        )(term_weights, left_environment)
    with jax.named_scope("left_over_z"):
        left_terms = list(pairs)
        for d in sorted(range(1, chips), key=lambda d: -min(d, chips - d)):
            route = [(p, (p + 2 * d) % layers) for p in range(layers)]
            left_terms[d] = lax.ppermute(pairs[d], "mpo", route)
        arrived, *left_terms = lax.optimization_barrier((arrived, *left_terms))
    with jax.named_scope("left_over_core"):
        given = pl.pallas_call(
            collect_kernel,
            out_shape=jax.ShapeDtypeStruct((chips, long, width), BF16),
            in_specs=[anywhere] * chips,
            out_specs=anywhere,
            scratch_shapes=[pltpu.SemaphoreType.DMA],
            compiler_params=pltpu.CompilerParams(vmem_limit_bytes=4 * MIB),
        )(*left_terms)
        taken = lax.ppermute(given, "mpo", [(p, p ^ 1) for p in range(layers)])
    with jax.named_scope("order"):
        ordered = pl.pallas_call(
            order_kernel,
            out_shape=jax.ShapeDtypeStruct((blocks, terms, width, width), BF16),
            in_specs=[scalars, anywhere],
            out_specs=anywhere,
            scratch_shapes=[pltpu.VMEM((blocks, terms, width, width), BF16), pltpu.SemaphoreType.DMA((blocks + 1,))],
            compiler_params=pltpu.CompilerParams(vmem_limit_bytes=60 * MIB),
        )(right_sector, arrived)
    with jax.named_scope("right_over_mpo"):
        right_terms = lax.all_to_all(ordered, "mpo", 0, 0, tiled=True)
    with jax.named_scope("lanczos"):
        vector = lax.dynamic_slice_in_dim(wavefunction, own, 1, 0)
        pieces = pl.pallas_call(
            lanczos_kernel,
            out_shape=jax.ShapeDtypeStruct((layers, 2 * rows + 8, width), F32),
            in_specs=[scalars, scalars, scalars, vmem, vmem, vmem] + [vmem] * chips,
            out_specs=vmem,
            compiler_params=pltpu.CompilerParams(vmem_limit_bytes=16 * MIB),
        )(left_size, right_size, right_sector, vector, right_terms, taken, *left_terms)
    with jax.named_scope("rows_over_mpo"):
        pieces = lax.all_to_all(pieces, "mpo", 0, 0, tiled=True)
    with jax.named_scope("numbers_over_sec"):
        line = jnp.sum(pieces[:, 2 * rows :, :], axis=0)
        shared = lax.all_to_all(jnp.broadcast_to(line[None], (devices, 8, width)), "sec", 0, 0, tiled=True)
    with jax.named_scope("finish"):
        own_rows = lax.dynamic_slice_in_dim(wavefunction, own * rows, rows, 1)
        next_vector, residual, coefficients = pl.pallas_call(
            finish_kernel,
            out_shape=(
                jax.ShapeDtypeStruct((blocks, rows, width), F32),
                jax.ShapeDtypeStruct((blocks, rows, width), F32),
                jax.ShapeDtypeStruct((1, width), F32),
            ),
            in_specs=[scalars, scalars, scalars, vmem, vmem, vmem],
            out_specs=(vmem, vmem, vmem),
            compiler_params=pltpu.CompilerParams(vmem_limit_bytes=8 * MIB),
        )(left_size, right_size, right_sector, own_rows, pieces, shared)
    return (next_vector, residual, coefficients[0, :3])


def solution(mesh):
    placed = (
        P("sec", None, None),
        P("sec"),
        P(),
        P(),
        P("mpo", "sec", None, None),
        P("mpo", "sec", None, None),
        P("mpo"),
    )
    return jax.shard_map(
        shards,
        mesh=mesh,
        in_specs=placed,
        out_specs=(P("sec", "mpo", None), P("sec", "mpo", None), P()),
        check_vma=False,
    )
```

```python
import jax
import jax.numpy as jnp
from jax import lax
from jax.experimental import pallas as pl
from jax.experimental.pallas import tpu as pltpu
from jax.sharding import PartitionSpec as P

F32 = jnp.float32
BF16 = jnp.bfloat16
SLOTS = 2
PAD = 16
LANES = 8
MIB = 1024 * 1024


def pack_right_kernel(right_sector, right_env, right_out, stage, sem):
    blocks = right_env.shape[1]
    devices = right_out.shape[0]
    sec = lax.axis_index("sec")
    load = pltpu.make_async_copy(right_env, stage, sem.at[0])
    load.start()
    picks = []
    for t in range(devices):
        first = jnp.int32(-1)
        last = jnp.int32(0)
        for i in range(blocks):
            sector = right_sector[t * blocks + i]
            match = sector // blocks == sec
            local = sector % blocks
            first = jnp.where(match & (first < 0), local, first)
            last = jnp.where(match, local, last)
        picks.append((jnp.maximum(first, 0), last))
    load.wait()
    copies = []
    for t in range(devices):
        for k in range(SLOTS):
            copies.append(pltpu.make_async_copy(stage.at[:, picks[t][k]], right_out.at[t, k], sem.at[1]))
            copies[-1].start()
    for copy in copies:
        copy.wait()


def pack_left_kernel(weights, left_env, *rest):
    *pairs, stage, wbuf, sem = rest
    terms, _, width, _ = left_env.shape
    chips = len(pairs)
    own = lax.axis_index("mpo")
    load = pltpu.make_async_copy(left_env, stage, sem.at[0])
    load.start()
    row = lax.broadcasted_iota(jnp.int32, wbuf.shape, 0)
    vals = jnp.zeros(wbuf.shape, F32)
    for w in range(terms):
        whole = jnp.full(wbuf.shape, weights[w], F32)
        high = whole.astype(BF16).astype(F32)
        mid = (whole - high).astype(BF16).astype(F32)
        low = whole - high - mid
        for j, part in enumerate((high, mid, low)):
            vals = jnp.where(row == w * 3 + j, part, vals)
    wbuf[...] = vals.astype(BF16)
    load.wait()
    copies = []
    for d, pair in enumerate(pairs):
        chip = (own // 2 + d) % chips
        for side in range(2):
            q = 2 * chip + (own % 2 + side) % 2
            for w in range(terms):
                rows = pl.ds((side * terms + w) * width, width)
                copies.append(pltpu.make_async_copy(stage.at[w, q], pair.at[rows], sem.at[1]))
        copies.append(pltpu.make_async_copy(wbuf, pair.at[pl.ds(2 * terms * width, PAD)], sem.at[1]))
    for copy in copies:
        copy.start()
    for copy in copies:
        copy.wait()


def collect_kernel(*refs):
    *pairs, given, sem = refs
    copies = []
    for d, pair in enumerate(pairs):
        rows = pl.ds(pair.shape[0] - given.shape[1], given.shape[1])
        copies.append(pltpu.make_async_copy(pair.at[rows], given.at[d], sem))
        copies[-1].start()
    for copy in copies:
        copy.wait()


def order_kernel(right_sector, arrived, ordered, stage, sem):
    blocks = ordered.shape[0]
    sec = lax.axis_index("sec")
    sources = [right_sector[sec * blocks + q] // blocks for q in range(blocks)]
    loads = []
    for q in range(blocks):
        again = jnp.bool_(False)
        for other in range(q):
            again = again | (sources[other] == sources[q])
        load = pltpu.make_async_copy(arrived.at[sources[q], jnp.where(again, 1, 0)], stage.at[q], sem.at[q])
        load.start()
        loads.append(load)
    stores = []
    for q in range(blocks):
        loads[q].wait()
        stores.append(pltpu.make_async_copy(stage.at[q], ordered.at[q], sem.at[blocks]))
        stores[-1].start()
    for store in stores:
        store.wait()


def live(rows, left, right):
    row = lax.broadcasted_iota(jnp.int32, rows, 0)
    col = lax.broadcasted_iota(jnp.int32, rows, 1)
    return (row < left) & (col < right)


def total(x):
    return jnp.sum(jnp.sum(x, axis=0, keepdims=True), axis=1, keepdims=True)


def lanczos_kernel(left_size, right_size, right_sector, vectors, right_terms, taken, *rest):
    *left_terms, out, vector, sem = rest
    sources, terms, width, _ = right_terms.shape
    chips = len(left_terms)
    sec = lax.axis_index("sec")
    own = lax.axis_index("mpo")
    blocks = left_size.shape[0]
    load = pltpu.make_async_copy(vectors.at[own], vector, sem)
    load.start()
    mask = live((width, width), left_size[own], right_size[right_sector[sec * blocks + own]])

    def apply(block):
        acc = jnp.zeros((width, width), F32)
        for move in range(sources):
            step, side = move // 2, move % 2
            source = 2 * ((own // 2 + chips - step) % chips) + (own % 2 + side) % 2
            part = left_terms[step] if side == 0 else taken.at[step]
            half = jnp.dot(part[: terms * width], block, preferred_element_type=F32)
            scale = part[part.shape[0] - PAD :].astype(F32)
            halves = []
            for w in range(terms):
                weight = scale[3 * w : 3 * w + 1] + scale[3 * w + 1 : 3 * w + 2] + scale[3 * w + 2 : 3 * w + 3]
                halves.append((weight * half[w * width : (w + 1) * width]).astype(BF16))
            rights = [right_terms[source, w] for w in range(terms)]
            acc = acc + lax.dot_general(
                jnp.concatenate(halves, axis=1),
                jnp.concatenate(rights, axis=1),
                (((1,), (1,)), ((), ())),
                preferred_element_type=F32,
            )
        return jnp.where(mask, acc, 0.0)

    load.wait()
    start = jnp.where(mask, vector[...].astype(F32), 0.0)
    norm = total(start * start)
    scale = 1.0 / jnp.sqrt(norm / float(width * width) + 1e-06)
    image = apply(start.astype(BF16)) * scale
    unit = start * scale
    length = total(unit * unit)
    overlap = total(unit * image)
    ratio = jnp.where(length > 0.0, overlap / jnp.where(length > 0.0, length, 1.0), 0.0)
    rest = image - ratio * unit
    after = apply(rest.astype(BF16))
    numbers = (
        norm,
        overlap,
        ratio,
        total(rest * rest),
        total(rest * after),
        total(unit * after) + total(rest * image),
        total(rest * unit),
    )
    lane = lax.broadcasted_iota(jnp.int32, (8, width), 1)
    line = jnp.zeros((8, width), F32)
    for j, number in enumerate(numbers):
        line = jnp.where(lane == own * LANES + j, number, line)
    parts = out.shape[0]
    rows = width // parts
    for d in range(parts):
        out[d, :rows] = rest[d * rows : (d + 1) * rows]
        out[d, rows : 2 * rows] = after[d * rows : (d + 1) * rows]
        out[d, 2 * rows :] = line


def finish_kernel(left_size, right_size, right_sector, vectors, pieces, shared, next_out, rest_out, coef_out, vector, sem):
    blocks, rows, width = next_out.shape
    sec = lax.axis_index("sec")
    part = lax.axis_index("mpo")
    devices = shared.shape[0]
    groups = PAD // rows
    load = pltpu.make_async_copy(vectors.at[:, pl.ds(pl.multiple_of(part // groups * PAD, PAD), PAD)], vector, sem)
    load.start()
    entries = float(devices * blocks * width * width)
    cells = float(width * width)
    stats = shared[:, 0, :]
    lane = lax.broadcasted_iota(jnp.int32, stats.shape, 1) % LANES

    def field(x, j):
        return x if j == 0 else pltpu.roll(x, x.shape[1] - j, 1)

    lead = lane == 0
    norm = jnp.where(lead, field(stats, 0), 0.0)
    overlap = field(stats, 1)
    ratio = field(stats, 2)
    gain = 1.0 / jnp.sqrt(total(norm) / entries + 1e-06)
    mean = jnp.where(lead, norm, 0.0) / cells + 1e-06
    weight = jnp.where(lead, (gain * gain) * mean, 0.0)
    length = norm / mean
    alpha = total(jnp.where(lead, weight * overlap, 0.0)) / entries
    delta = jnp.where(lead, ratio - alpha, 0.0)
    rest_total = total(jnp.where(lead, weight * (field(stats, 3) + delta * delta * length + 2.0 * delta * field(stats, 6)), 0.0))
    beta = jnp.sqrt(rest_total / entries + 1e-06)
    inner = field(stats, 4) + delta * field(stats, 5) + delta * delta * overlap
    alpha_next = total(jnp.where(lead, weight * inner, 0.0)) / entries / beta / beta
    for j, number in enumerate((alpha, beta, alpha_next)):
        coef_out[j] = number[0, 0]
    load.wait()
    for q in range(blocks):
        line = pieces[q, 2 * rows : 2 * rows + 1, :]
        lane_one = lax.broadcasted_iota(jnp.int32, line.shape, 1)
        norm_q = jnp.sum(jnp.where(lane_one == q * LANES, line, 0.0), axis=1, keepdims=True)
        ratio_q = jnp.sum(jnp.where(lane_one == q * LANES + 2, line, 0.0), axis=1, keepdims=True)
        root = jnp.sqrt(norm_q / cells + 1e-06)
        scale = gain * root
        row = lax.broadcasted_iota(jnp.int32, (rows, width), 0) + part * rows
        col = lax.broadcasted_iota(jnp.int32, (rows, width), 1)
        mask = (row < left_size[q]) & (col < right_size[right_sector[sec * blocks + q]])
        group = vector[q].astype(F32)
        own_rows = group[:rows]
        for j in range(1, groups):
            own_rows = jnp.where(part % groups == j, group[j * rows : (j + 1) * rows], own_rows)
        unit = jnp.where(mask, own_rows, 0.0) / root
        rest = pieces[q, :rows]
        after = pieces[q, rows : 2 * rows]
        shift = ratio_q - alpha
        second = (scale / beta) * (rest + shift * unit)
        image = (scale / beta) * (after + shift * (rest + ratio_q * unit))
        next_out[q] = second
        rest_out[q] = image - alpha_next * second - (beta * scale) * unit


def shards(
    wavefunction,
    left_size,
    right_size,
    right_sector,
    left_environment,
    right_environment,
    term_weights,
):
    blocks, width, _ = wavefunction.shape
    terms = left_environment.shape[0]
    devices = lax.axis_size("sec")
    layers = lax.axis_size("mpo")
    rows = width // layers
    anywhere = pl.BlockSpec(memory_space=pl.ANY)
    scalars = pl.BlockSpec(memory_space=pltpu.SMEM)
    vmem = pl.BlockSpec(memory_space=pltpu.VMEM)

    chips = layers // 2
    long = terms * width + PAD
    with jax.named_scope("pack_right"):
        right_out = pl.pallas_call(
            pack_right_kernel,
            out_shape=jax.ShapeDtypeStruct((devices, SLOTS, terms, width, width), BF16),
            in_specs=[scalars, anywhere],
            out_specs=anywhere,
            scratch_shapes=[pltpu.VMEM(right_environment.shape, BF16), pltpu.SemaphoreType.DMA((2,))],
            compiler_params=pltpu.CompilerParams(vmem_limit_bytes=60 * MIB),
        )(right_sector, right_environment)
    with jax.named_scope("right_over_sec"):
        arrived = lax.all_to_all(right_out, "sec", 0, 0, tiled=True)
    with jax.named_scope("pack_left"):
        pairs = pl.pallas_call(
            pack_left_kernel,
            out_shape=(jax.ShapeDtypeStruct((terms * width + long, width), BF16),) * chips,
            in_specs=[scalars, anywhere],
            out_specs=(anywhere,) * chips,
            scratch_shapes=[
                pltpu.VMEM(left_environment.shape, BF16),
                pltpu.VMEM((PAD, width), BF16),
                pltpu.SemaphoreType.DMA((2,)),
            ],
            compiler_params=pltpu.CompilerParams(vmem_limit_bytes=8 * MIB),
        )(term_weights, left_environment)
    with jax.named_scope("left_over_z"):
        left_terms = list(pairs)
        for d in sorted(range(1, chips), key=lambda d: -min(d, chips - d)):
            route = [(p, (p + 2 * d) % layers) for p in range(layers)]
            left_terms[d] = lax.ppermute(pairs[d], "mpo", route)
        arrived, left_terms[4] = lax.optimization_barrier((arrived, left_terms[4]))
    with jax.named_scope("order"):
        ordered = pl.pallas_call(
            order_kernel,
            out_shape=jax.ShapeDtypeStruct((blocks, terms, width, width), BF16),
            in_specs=[scalars, anywhere],
            out_specs=anywhere,
            scratch_shapes=[pltpu.VMEM((blocks, terms, width, width), BF16), pltpu.SemaphoreType.DMA((blocks + 1,))],
            compiler_params=pltpu.CompilerParams(vmem_limit_bytes=60 * MIB),
        )(right_sector, arrived)
        ordered, left_terms[3], left_terms[5], left_terms[2], left_terms[6], left_terms[1], left_terms[7] = lax.optimization_barrier((ordered, left_terms[3], left_terms[5], left_terms[2], left_terms[6], left_terms[1], left_terms[7]))
    with jax.named_scope("left_over_core"):
        given = pl.pallas_call(
            collect_kernel,
            out_shape=jax.ShapeDtypeStruct((chips, long, width), BF16),
            in_specs=[anywhere] * chips,
            out_specs=anywhere,
            scratch_shapes=[pltpu.SemaphoreType.DMA],
            compiler_params=pltpu.CompilerParams(vmem_limit_bytes=4 * MIB),
        )(*left_terms)
        taken = lax.ppermute(given, "mpo", [(p, p ^ 1) for p in range(layers)])
    with jax.named_scope("right_over_mpo"):
        right_terms = lax.all_to_all(ordered, "mpo", 0, 0, tiled=True)
    with jax.named_scope("lanczos"):
        pieces = pl.pallas_call(
            lanczos_kernel,
            out_shape=jax.ShapeDtypeStruct((layers, 2 * rows + 8, width), F32),
            in_specs=[scalars, scalars, scalars, anywhere, vmem, vmem] + [vmem] * chips,
            out_specs=vmem,
            scratch_shapes=[pltpu.VMEM((width, width), BF16), pltpu.SemaphoreType.DMA],
            compiler_params=pltpu.CompilerParams(vmem_limit_bytes=16 * MIB),
        )(left_size, right_size, right_sector, wavefunction, right_terms, taken, *left_terms)
    with jax.named_scope("rows_over_mpo"):
        pieces = lax.all_to_all(pieces, "mpo", 0, 0, tiled=True)
    with jax.named_scope("numbers_over_sec"):
        line = jnp.sum(pieces[:, 2 * rows :, :], axis=0)
        shared = lax.all_to_all(jnp.broadcast_to(line[None], (devices, 8, width)), "sec", 0, 0, tiled=True)
    with jax.named_scope("finish"):
        next_vector, residual, coefficients = pl.pallas_call(
            finish_kernel,
            out_shape=(
                jax.ShapeDtypeStruct((blocks, rows, width), F32),
                jax.ShapeDtypeStruct((blocks, rows, width), F32),
                jax.ShapeDtypeStruct((3,), F32),
            ),
            in_specs=[scalars, scalars, scalars, anywhere, vmem, vmem],
            out_specs=(vmem, vmem, scalars),
            scratch_shapes=[pltpu.VMEM((blocks, PAD, width), BF16), pltpu.SemaphoreType.DMA],
            compiler_params=pltpu.CompilerParams(vmem_limit_bytes=8 * MIB),
        )(left_size, right_size, right_sector, wavefunction, pieces, shared)
    return (next_vector, residual, coefficients)


def solution(mesh):
    placed = (
        P("sec", None, None),
        P("sec"),
        P(),
        P(),
        P("mpo", "sec", None, None),
        P("mpo", "sec", None, None),
        P("mpo"),
    )
    return jax.shard_map(
        shards,
        mesh=mesh,
        in_specs=placed,
        out_specs=(P("sec", "mpo", None), P("sec", "mpo", None), P()),
        check_vma=False,
    )
```

```python
import jax
import jax.numpy as jnp
from jax import lax
from jax.experimental import pallas as pl
from jax.experimental.pallas import tpu as pltpu
from jax.sharding import PartitionSpec as P

F32 = jnp.float32
BF16 = jnp.bfloat16
SLOTS = 2
PAD = 16
LANES = 8
MIB = 1024 * 1024


def sector_of(chip, core, kind, chips):
    cuts = chips // 2
    return ((chip + chips - 1 - kind) % cuts) * 4 + kind * 2 + core


MOVES = ((0, (0, 1)), (2, (1,)), (-2, (0,)), (1, (0, 1)), (-1, (0, 1)))


def targets(own, chips):
    chip, core = own // 2, own % 2
    return [
        [sector_of((chip + move + chips) % chips, (core + side) % 2, kind, chips) for side in range(2) for kind in kinds]
        for move, kinds in MOVES
    ]


def parts_of(kind):
    found = []
    base = 0
    for index, (_, kinds) in enumerate(MOVES):
        if kind in kinds:
            found.append((index, kinds.index(kind), base + kinds.index(kind)))
        base += len(kinds)
    return found


def start_all(copies):
    for copy in copies:
        copy.start()
    for copy in copies:
        copy.wait()


def pack_right_kernel(right_sector, right_env, right_out, stage, sem):
    blocks = right_env.shape[1]
    devices = right_out.shape[0]
    sec = lax.axis_index("sec")
    load = pltpu.make_async_copy(right_env, stage, sem.at[0])
    load.start()
    base = sec * blocks
    picks = []
    copies = []
    for t in range(devices):
        first = jnp.int32(blocks * blocks)
        last = jnp.int32(0)
        for i in range(blocks):
            offset = right_sector[t * blocks + i] - base
            match = (offset >= 0) & (offset < blocks)
            first = jnp.where(match, jnp.minimum(first, offset + i * blocks), first)
            last = jnp.where(match, offset, last)
        picks.append((first & (blocks - 1), last))
        if t < devices // 4:
            continue
        if t == devices // 4:
            load.wait()
        for ready in range(t + 1 if t == devices // 4 else 1):
            target = ready if t == devices // 4 else t
            for k in range(SLOTS):
                copies.append(pltpu.make_async_copy(stage.at[:, picks[target][k]], right_out.at[target, k], sem.at[1]))
                copies[-1].start()
    for copy in copies:
        copy.wait()


def pack_left_kernel(weights, left_env, *rest):
    *lefts, stage, wbuf, sem = rest
    terms, _, width, _ = left_env.shape
    own = lax.axis_index("mpo")
    load = pltpu.make_async_copy(left_env, stage, sem.at[0])
    load.start()
    row = lax.broadcasted_iota(jnp.int32, wbuf.shape, 0)
    vals = jnp.zeros(wbuf.shape, F32)
    for w in range(terms):
        whole = jnp.full(wbuf.shape, weights[w], F32)
        high = whole.astype(BF16).astype(F32)
        mid = (whole - high).astype(BF16).astype(F32)
        low = whole - high - mid
        for j, part in enumerate((high, mid, low)):
            vals = jnp.where(row == w * 3 + j, part, vals)
    wbuf[...] = vals.astype(BF16)
    load.wait()
    copies = []
    for left, sectors in zip(lefts, targets(own, lax.axis_size("mpo") // 2)):
        for place, q in enumerate(sectors):
            for w in range(terms):
                rows = pl.ds((place * terms + w) * width, width)
                copies.append(pltpu.make_async_copy(stage.at[w, q], left.at[rows], sem.at[1]))
        copies.append(pltpu.make_async_copy(wbuf, left.at[pl.ds(len(sectors) * terms * width, PAD)], sem.at[1]))
    start_all(copies)


def collect_left_kernel(*refs):
    *lefts, given, sem = refs
    size = given.shape[1] - PAD
    copies = []
    place = 0
    for left, (_, kinds) in zip(lefts, MOVES):
        for j in range(len(kinds)):
            rows = pl.ds((len(kinds) + j) * size, size)
            copies.append(pltpu.make_async_copy(left.at[rows], given.at[place, pl.ds(0, size)], sem))
            pad = pl.ds(2 * len(kinds) * size, PAD)
            copies.append(pltpu.make_async_copy(left.at[pad], given.at[place, pl.ds(size, PAD)], sem))
            place += 1
    start_all(copies)


def collect_right_kernel(*refs):
    *rights, given, sem = refs
    copies = []
    place = 0
    for right, (_, kinds) in zip(rights, MOVES):
        count = len(kinds)
        copies.append(pltpu.make_async_copy(right.at[pl.ds(count, count)], given.at[pl.ds(place, count)], sem))
        place += count
    start_all(copies)


def order_kernel(right_sector, arrived, *rest):
    *rights, stage, places, sem = rest
    blocks = stage.shape[0]
    sec = lax.axis_index("sec")
    own = lax.axis_index("mpo")
    shift = blocks.bit_length() - 1
    sources = [lax.shift_right_logical(right_sector[sec * blocks + q], shift) for q in range(blocks)]
    for q in range(blocks):
        again = jnp.bool_(False)
        for other in range(q):
            again = again | (sources[other] == sources[q])
        places[q] = sources[q] * SLOTS + jnp.where(again, 1, 0)
    loads = []
    for sectors in targets(own, lax.axis_size("mpo") // 2):
        for q in sectors:
            index = len(loads)
            load = pltpu.make_async_copy(arrived.at[places[q]], stage.at[index], sem.at[index])
            load.start()
            loads.append(load)
    stores = []
    first = 0
    for right in rights:
        count = right.shape[0]
        for index in range(first, first + count):
            loads[index].wait()
        stores.append(pltpu.make_async_copy(stage.at[pl.ds(first, count)], right, sem.at[blocks]))
        stores[-1].start()
        first += count
    for store in stores:
        store.wait()


def live(rows, left, right):
    row = lax.broadcasted_iota(jnp.int32, rows, 0)
    col = lax.broadcasted_iota(jnp.int32, rows, 1)
    return (row < left) & (col < right)


def total(x):
    return jnp.sum(jnp.sum(x, axis=0, keepdims=True), axis=1, keepdims=True)


def apply(block, kind, lefts, given_left, rights, given_right):
    _, terms, width, _ = given_right.shape
    size = terms * width
    acc = jnp.zeros((width, width), F32)
    for index, place, other in parts_of(kind):
        for side in range(2):
            if side == 0:
                left = lefts[index][place * size : (place + 1) * size]
                scale = lefts[index][lefts[index].shape[0] - PAD :].astype(F32)
                right = [rights[index][place, w] for w in range(terms)]
            else:
                left = given_left[other, :size]
                scale = given_left[other, size:].astype(F32)
                right = [given_right[other, w] for w in range(terms)]
            half = jnp.dot(left, block, preferred_element_type=F32)
            halves = []
            for w in range(terms):
                weight = scale[3 * w : 3 * w + 1] + scale[3 * w + 1 : 3 * w + 2] + scale[3 * w + 2 : 3 * w + 3]
                halves.append((weight * half[w * width : (w + 1) * width]).astype(BF16))
            acc = acc + lax.dot_general(
                jnp.concatenate(halves, axis=1),
                jnp.concatenate(right, axis=1),
                (((1,), (1,)), ((), ())),
                preferred_element_type=F32,
            )
    return acc


def own_sector(kind):
    own = lax.axis_index("mpo")
    return sector_of(own // 2, own % 2, kind, lax.axis_size("mpo") // 2)


def start_vector(kind, left_size, right_size, right_sector, vector):
    width = vector.shape[1]
    q = own_sector(kind)
    sec = lax.axis_index("sec")
    mask = live((width, width), left_size[q], right_size[right_sector[sec * left_size.shape[0] + q]])
    return mask, jnp.where(mask, vector[kind].astype(F32), 0.0)


def load_vectors(vectors, vector, sem):
    start_all([pltpu.make_async_copy(vectors.at[own_sector(kind)], vector.at[kind], sem) for kind in range(2)])


def first_kernel(left_size, right_size, right_sector, vectors, *rest):
    *blocks, out, vector, sem = rest
    half = len(blocks) // 2
    lefts, rights = blocks[: half - 1], blocks[half:-1]
    load_vectors(vectors, vector, sem)
    for kind in range(2):
        _, start = start_vector(kind, left_size, right_size, right_sector, vector)
        out[kind] = apply(start.astype(BF16), kind, lefts, blocks[half - 1], rights, blocks[-1])


def second_kernel(left_size, right_size, right_sector, vectors, image_here, image_there, *rest):
    *blocks, out, vector, sem = rest
    half = len(blocks) // 2
    lefts, rights = blocks[: half - 1], blocks[half:-1]
    width = vector.shape[1]
    upper = lax.axis_index("mpo") // 2 >= lax.axis_size("mpo") // 4
    load_vectors(vectors, vector, sem)
    parts = out.shape[0]
    rows = width // parts
    lane = lax.broadcasted_iota(jnp.int32, (8, width), 1)
    line = jnp.zeros((8, width), F32)
    rests = []
    for kind in range(2):
        mask, start = start_vector(kind, left_size, right_size, right_sector, vector)
        norm = total(start * start)
        scale = 1.0 / jnp.sqrt(norm / float(width * width) + 1e-06)
        image = jnp.where(mask, image_here[kind] + image_there[kind], 0.0) * scale
        unit = start * scale
        length = total(unit * unit)
        overlap = total(unit * image)
        ratio = jnp.where(length > 0.0, overlap / jnp.where(length > 0.0, length, 1.0), 0.0)
        rest = image - ratio * unit
        after = jnp.where(mask, apply(rest.astype(BF16), kind, lefts, blocks[half - 1], rights, blocks[-1]), 0.0)
        share = jnp.where(upper == (kind == 1), 1.0, 0.0)
        numbers = (
            share * norm,
            share * overlap,
            share * ratio,
            share * total(rest * rest),
            total(rest * after),
            total(unit * after) + share * total(rest * image),
            share * total(rest * unit),
        )
        place = own_sector(kind) * LANES
        for j, number in enumerate(numbers):
            line = jnp.where(lane == place + j, number, line)
        rests.append(rest)
        for d in range(parts):
            out[d, (1 + kind) * rows : (2 + kind) * rows] = after[d * rows : (d + 1) * rows]
    chosen = jnp.where(upper, rests[1], rests[0])
    for d in range(parts):
        out[d, :rows] = chosen[d * rows : (d + 1) * rows]
        out[d, 3 * rows :] = line


def finish_kernel(left_size, right_size, right_sector, vectors, pieces, shared, next_out, rest_out, coef_out, vector, sem):
    blocks, rows, width = next_out.shape
    sec = lax.axis_index("sec")
    part = lax.axis_index("mpo")
    devices = shared.shape[0]
    groups = PAD // rows
    load = pltpu.make_async_copy(vectors.at[:, pl.ds(pl.multiple_of(part // groups * PAD, PAD), PAD)], vector, sem)
    load.start()
    entries = float(devices * blocks * width * width)
    cells = float(width * width)
    stats = shared[:, 0, :]
    line = shared[sec][:1]
    chips = lax.axis_size("mpo") // 2
    lane = lax.broadcasted_iota(jnp.int32, stats.shape, 1) % LANES

    def field(x, j):
        return x if j == 0 else pltpu.roll(x, x.shape[1] - j, 1)

    lead = lane == 0
    norm = jnp.where(lead, field(stats, 0), 0.0)
    overlap = field(stats, 1)
    ratio = field(stats, 2)
    gain = 1.0 / jnp.sqrt(total(norm) / entries + 1e-06)
    mean = jnp.where(lead, norm, 0.0) / cells + 1e-06
    weight = jnp.where(lead, (gain * gain) * mean, 0.0)
    length = norm / mean
    alpha = total(jnp.where(lead, weight * overlap, 0.0)) / entries
    delta = jnp.where(lead, ratio - alpha, 0.0)
    rest_total = total(jnp.where(lead, weight * (field(stats, 3) + delta * delta * length + 2.0 * delta * field(stats, 6)), 0.0))
    beta = jnp.sqrt(rest_total / entries + 1e-06)
    inner = field(stats, 4) + delta * field(stats, 5) + delta * delta * overlap
    alpha_next = total(jnp.where(lead, weight * inner, 0.0)) / entries / beta / beta
    for j, number in enumerate((alpha, beta, alpha_next)):
        coef_out[j] = number[0, 0]
    load.wait()
    for q in range(blocks):
        cut, kind, core = q // 4, q // 2 % 2, q % 2
        lower = 2 * ((cut + 1 + kind) % (chips // 2)) + core
        higher = lower + chips
        lane_one = lax.broadcasted_iota(jnp.int32, line.shape, 1)
        norm_q = jnp.sum(jnp.where(lane_one == q * LANES, line, 0.0), axis=1, keepdims=True)
        ratio_q = jnp.sum(jnp.where(lane_one == q * LANES + 2, line, 0.0), axis=1, keepdims=True)
        root = jnp.sqrt(norm_q / cells + 1e-06)
        scale = gain * root
        row = lax.broadcasted_iota(jnp.int32, (rows, width), 0) + part * rows
        col = lax.broadcasted_iota(jnp.int32, (rows, width), 1)
        mask = (row < left_size[q]) & (col < right_size[right_sector[sec * blocks + q]])
        group = vector[q].astype(F32)
        own_rows = group[:rows]
        for j in range(1, groups):
            own_rows = jnp.where(part % groups == j, group[j * rows : (j + 1) * rows], own_rows)
        unit = jnp.where(mask, own_rows, 0.0) / root
        rest = pieces[higher if kind else lower, :rows]
        after_rows = slice((1 + kind) * rows, (2 + kind) * rows)
        after = pieces[lower, after_rows] + pieces[higher, after_rows]
        shift = ratio_q - alpha
        second = (scale / beta) * (rest + shift * unit)
        image = (scale / beta) * (after + shift * (rest + ratio_q * unit))
        next_out[q] = second
        rest_out[q] = image - alpha_next * second - (beta * scale) * unit


def shards(
    wavefunction,
    left_size,
    right_size,
    right_sector,
    left_environment,
    right_environment,
    term_weights,
):
    blocks, width, _ = wavefunction.shape
    terms = left_environment.shape[0]
    devices = lax.axis_size("sec")
    layers = lax.axis_size("mpo")
    rows = width // layers
    anywhere = pl.BlockSpec(memory_space=pl.ANY)
    scalars = pl.BlockSpec(memory_space=pltpu.SMEM)
    vmem = pl.BlockSpec(memory_space=pltpu.VMEM)

    chips = layers // 2
    long = terms * width
    routes = [[(p, (p + 2 * move) % layers) for p in range(layers)] for move, _ in MOVES]
    counts = [2 * len(kinds) for _, kinds in MOVES]
    cores = [(p, p ^ 1) for p in range(layers)]
    with jax.named_scope("pack_right"):
        right_out = pl.pallas_call(
            pack_right_kernel,
            out_shape=jax.ShapeDtypeStruct((devices, SLOTS, terms, width, width), BF16),
            in_specs=[scalars, anywhere],
            out_specs=anywhere,
            scratch_shapes=[pltpu.VMEM(right_environment.shape, BF16), pltpu.SemaphoreType.DMA((2,))],
            compiler_params=pltpu.CompilerParams(vmem_limit_bytes=60 * MIB),
        )(right_sector, right_environment)
    with jax.named_scope("right_over_sec"):
        arrived = lax.all_to_all(right_out, "sec", 0, 0, tiled=True)
    with jax.named_scope("pack_left"):
        lefts = pl.pallas_call(
            pack_left_kernel,
            out_shape=[jax.ShapeDtypeStruct((count * long + PAD, width), BF16) for count in counts],
            in_specs=[scalars, anywhere],
            out_specs=[anywhere] * len(MOVES),
            scratch_shapes=[
                pltpu.VMEM(left_environment.shape, BF16),
                pltpu.VMEM((PAD, width), BF16),
                pltpu.SemaphoreType.DMA((2,)),
            ],
            compiler_params=pltpu.CompilerParams(vmem_limit_bytes=8 * MIB),
        )(term_weights, left_environment)
    with jax.named_scope("left_over_z"):
        lefts = [lefts[0]] + [lax.ppermute(left, "mpo", route) for left, route in zip(lefts[1:], routes[1:])]
    with jax.named_scope("left_over_core"):
        given = pl.pallas_call(
            collect_left_kernel,
            out_shape=jax.ShapeDtypeStruct((blocks // 2, long + PAD, width), BF16),
            in_specs=[anywhere] * len(MOVES),
            out_specs=anywhere,
            scratch_shapes=[pltpu.SemaphoreType.DMA],
            compiler_params=pltpu.CompilerParams(vmem_limit_bytes=4 * MIB),
        )(*lefts)
        lefts.append(lax.ppermute(given, "mpo", cores))
        arrived, *lefts = lax.optimization_barrier((arrived, *lefts))
    with jax.named_scope("order"):
        rights = pl.pallas_call(
            order_kernel,
            out_shape=[jax.ShapeDtypeStruct((count, terms, width, width), BF16) for count in counts],
            in_specs=[scalars, anywhere],
            out_specs=[anywhere] * len(MOVES),
            scratch_shapes=[
                pltpu.VMEM((blocks, terms, width, width), BF16),
                pltpu.SMEM((blocks,), jnp.int32),
                pltpu.SemaphoreType.DMA((blocks + 1,)),
            ],
            compiler_params=pltpu.CompilerParams(vmem_limit_bytes=60 * MIB),
        )(right_sector, arrived.reshape(devices * SLOTS, terms, width, width))
    with jax.named_scope("right_over_z"):
        rights = [rights[0]] + [lax.ppermute(right, "mpo", route) for right, route in zip(rights[1:], routes[1:])]
    with jax.named_scope("right_over_core"):
        given = pl.pallas_call(
            collect_right_kernel,
            out_shape=jax.ShapeDtypeStruct((blocks // 2, terms, width, width), BF16),
            in_specs=[anywhere] * len(MOVES),
            out_specs=anywhere,
            scratch_shapes=[pltpu.SemaphoreType.DMA],
            compiler_params=pltpu.CompilerParams(vmem_limit_bytes=4 * MIB),
        )(*rights)
        rights.append(lax.ppermute(given, "mpo", cores))
    with jax.named_scope("first_image"):
        image_here = pl.pallas_call(
            first_kernel,
            out_shape=jax.ShapeDtypeStruct((2, width, width), F32),
            in_specs=[scalars, scalars, scalars, anywhere] + [vmem] * (2 * len(MOVES) + 2),
            out_specs=vmem,
            scratch_shapes=[pltpu.VMEM((2, width, width), BF16), pltpu.SemaphoreType.DMA],
            compiler_params=pltpu.CompilerParams(vmem_limit_bytes=16 * MIB),
        )(left_size, right_size, right_sector, wavefunction, *lefts, *rights)
    with jax.named_scope("swap_images"):
        image_there = lax.ppermute(image_here, "mpo", [(p, (p + chips) % layers) for p in range(layers)])
    with jax.named_scope("second_image"):
        pieces = pl.pallas_call(
            second_kernel,
            out_shape=jax.ShapeDtypeStruct((layers, 3 * rows + 8, width), F32),
            in_specs=[scalars, scalars, scalars, anywhere] + [vmem] * (2 * len(MOVES) + 4),
            out_specs=vmem,
            scratch_shapes=[pltpu.VMEM((2, width, width), BF16), pltpu.SemaphoreType.DMA],
            compiler_params=pltpu.CompilerParams(vmem_limit_bytes=16 * MIB),
        )(left_size, right_size, right_sector, wavefunction, image_here, image_there, *lefts, *rights)
    with jax.named_scope("rows_over_mpo"):
        pieces = lax.all_to_all(pieces, "mpo", 0, 0, tiled=True)
    with jax.named_scope("numbers_over_sec"):
        line = jnp.sum(pieces[:, 3 * rows :, :], axis=0)
        shared = lax.all_to_all(jnp.broadcast_to(line[None], (devices, 8, width)), "sec", 0, 0, tiled=True)
    with jax.named_scope("finish"):
        next_vector, residual, coefficients = pl.pallas_call(
            finish_kernel,
            out_shape=(
                jax.ShapeDtypeStruct((blocks, rows, width), F32),
                jax.ShapeDtypeStruct((blocks, rows, width), F32),
                jax.ShapeDtypeStruct((3,), F32),
            ),
            in_specs=[scalars, scalars, scalars, anywhere, vmem, vmem],
            out_specs=(vmem, vmem, scalars),
            scratch_shapes=[pltpu.VMEM((blocks, PAD, width), BF16), pltpu.SemaphoreType.DMA],
            compiler_params=pltpu.CompilerParams(vmem_limit_bytes=8 * MIB),
        )(left_size, right_size, right_sector, wavefunction, pieces, shared)
    return (next_vector, residual, coefficients)


def solution(mesh):
    placed = (
        P("sec", None, None),
        P("sec"),
        P(),
        P(),
        P("mpo", "sec", None, None),
        P("mpo", "sec", None, None),
        P("mpo"),
    )
    return jax.shard_map(
        shards,
        mesh=mesh,
        in_specs=placed,
        out_specs=(P("sec", "mpo", None), P("sec", "mpo", None), P()),
        check_vma=False,
    )
```

```python
import jax
import jax.numpy as jnp
from jax import lax
from jax.experimental import pallas as pl
from jax.experimental.pallas import tpu as pltpu
from jax.sharding import PartitionSpec as P

F32 = jnp.float32
BF16 = jnp.bfloat16
SLOTS = 2
PAD = 16
LANES = 8
MIB = 1024 * 1024


def sector_of(chip, core, kind, chips):
    cuts = chips // 2
    return ((chip + chips - 1 - kind) % cuts) * 4 + kind * 2 + core


MOVES = ((0, (0, 1)), (2, (1,)), (-2, (0,)), (1, (0, 1)), (-1, (0, 1)))


def targets(own, chips):
    chip, core = own // 2, own % 2
    return [
        [sector_of((chip + move + chips) % chips, (core + side) % 2, kind, chips) for side in range(2) for kind in kinds]
        for move, kinds in MOVES
    ]


def parts_of(kind):
    found = []
    base = 0
    for index, (_, kinds) in enumerate(MOVES):
        if kind in kinds:
            found.append((index, kinds.index(kind), base + kinds.index(kind)))
        base += len(kinds)
    return found


def start_all(copies):
    for copy in copies:
        copy.start()
    for copy in copies:
        copy.wait()


def pack_right_kernel(right_sector, right_env, right_out, stage, sem):
    blocks = right_env.shape[1]
    devices = right_out.shape[0]
    sec = lax.axis_index("sec")
    load = pltpu.make_async_copy(right_env, stage, sem.at[0])
    load.start()
    base = sec * blocks
    picks = []
    copies = []
    for t in range(devices):
        first = jnp.int32(blocks * blocks)
        last = jnp.int32(0)
        for i in range(blocks):
            offset = right_sector[t * blocks + i] - base
            match = (offset >= 0) & (offset < blocks)
            first = jnp.where(match, jnp.minimum(first, offset + i * blocks), first)
            last = jnp.where(match, offset, last)
        picks.append((first & (blocks - 1), last))
        if t < devices // 4:
            continue
        if t == devices // 4:
            load.wait()
        for ready in range(t + 1 if t == devices // 4 else 1):
            target = ready if t == devices // 4 else t
            for k in range(SLOTS):
                copies.append(pltpu.make_async_copy(stage.at[:, picks[target][k]], right_out.at[target, k], sem.at[1]))
                copies[-1].start()
    for copy in copies:
        copy.wait()


def pack_left_kernel(weights, left_env, *rest):
    *lefts, stage, wbuf, sem = rest
    terms, _, width, _ = left_env.shape
    own = lax.axis_index("mpo")
    load = pltpu.make_async_copy(left_env, stage, sem.at[0])
    load.start()
    row = lax.broadcasted_iota(jnp.int32, wbuf.shape, 0)
    vals = jnp.zeros(wbuf.shape, F32)
    for w in range(terms):
        whole = jnp.full(wbuf.shape, weights[w], F32)
        high = whole.astype(BF16).astype(F32)
        mid = (whole - high).astype(BF16).astype(F32)
        low = whole - high - mid
        for j, part in enumerate((high, mid, low)):
            vals = jnp.where(row == w * 3 + j, part, vals)
    wbuf[...] = vals.astype(BF16)
    load.wait()
    copies = []
    for left, sectors in zip(lefts, targets(own, lax.axis_size("mpo") // 2)):
        for place, q in enumerate(sectors):
            for w in range(terms):
                rows = pl.ds((place * terms + w) * width, width)
                copies.append(pltpu.make_async_copy(stage.at[w, q], left.at[rows], sem.at[1]))
        copies.append(pltpu.make_async_copy(wbuf, left.at[pl.ds(len(sectors) * terms * width, PAD)], sem.at[1]))
    start_all(copies)


def collect_left_kernel(*refs):
    *lefts, given, sem = refs
    size = given.shape[1] - PAD
    copies = []
    place = 0
    for left, (_, kinds) in zip(lefts, MOVES):
        for j in range(len(kinds)):
            rows = pl.ds((len(kinds) + j) * size, size)
            copies.append(pltpu.make_async_copy(left.at[rows], given.at[place, pl.ds(0, size)], sem))
            pad = pl.ds(2 * len(kinds) * size, PAD)
            copies.append(pltpu.make_async_copy(left.at[pad], given.at[place, pl.ds(size, PAD)], sem))
            place += 1
    start_all(copies)


def collect_right_kernel(*refs):
    *rights, given, sem = refs
    copies = []
    place = 0
    for right, (_, kinds) in zip(rights, MOVES[1:]):
        count = len(kinds)
        copies.append(pltpu.make_async_copy(right.at[pl.ds(count, count)], given.at[pl.ds(place, count)], sem))
        place += count
    start_all(copies)


def order_kernel(right_sector, arrived, *rest):
    *rights, stage, places, sem = rest
    blocks = stage.shape[0]
    sec = lax.axis_index("sec")
    own = lax.axis_index("mpo")
    shift = blocks.bit_length() - 1
    sources = [lax.shift_right_logical(right_sector[sec * blocks + q], shift) for q in range(blocks)]
    for q in range(blocks):
        again = jnp.bool_(False)
        for other in range(q):
            again = again | (sources[other] == sources[q])
        places[q] = sources[q] * SLOTS + jnp.where(again, 1, 0)
    loads = []
    for sectors in targets(own, lax.axis_size("mpo") // 2):
        for q in sectors:
            index = len(loads)
            load = pltpu.make_async_copy(arrived.at[places[q]], stage.at[index], sem.at[index])
            load.start()
            loads.append(load)
    stores = []
    first = 0
    for right in rights:
        count = right.shape[0]
        for index in range(first, first + count):
            loads[index].wait()
        stores.append(pltpu.make_async_copy(stage.at[pl.ds(first, count)], right, sem.at[blocks]))
        stores[-1].start()
        first += count
    for store in stores:
        store.wait()


def live(rows, left, right):
    row = lax.broadcasted_iota(jnp.int32, rows, 0)
    col = lax.broadcasted_iota(jnp.int32, rows, 1)
    return (row < left) & (col < right)


def total(x):
    return jnp.sum(jnp.sum(x, axis=0, keepdims=True), axis=1, keepdims=True)


def apply(block, kind, lefts, given_left, rights, given_right):
    _, terms, width, _ = given_right.shape
    size = terms * width
    acc = jnp.zeros((width, width), F32)
    for index, place, other in reversed(parts_of(kind)):
        for side in range(2):
            if side == 0:
                left = lefts[index][place * size : (place + 1) * size]
                scale = lefts[index][lefts[index].shape[0] - PAD :].astype(F32)
                right = [rights[index + 1 if index else 0][place, w] for w in range(terms)]
            else:
                left = given_left[other, :size]
                scale = given_left[other, size:].astype(F32)
                right = [rights[1][place, w] if index == 0 else given_right[other - 2, w] for w in range(terms)]
            half = jnp.dot(left, block, preferred_element_type=F32)
            halves = []
            for w in range(terms):
                weight = scale[3 * w : 3 * w + 1] + scale[3 * w + 1 : 3 * w + 2] + scale[3 * w + 2 : 3 * w + 3]
                halves.append((weight * half[w * width : (w + 1) * width]).astype(BF16))
            acc = acc + lax.dot_general(
                jnp.concatenate(halves, axis=1),
                jnp.concatenate(right, axis=1),
                (((1,), (1,)), ((), ())),
                preferred_element_type=F32,
            )
    return acc


def own_sector(kind):
    own = lax.axis_index("mpo")
    return sector_of(own // 2, own % 2, kind, lax.axis_size("mpo") // 2)


def start_vector(kind, left_size, right_size, right_sector, vector):
    width = vector.shape[1]
    q = own_sector(kind)
    sec = lax.axis_index("sec")
    mask = live((width, width), left_size[q], right_size[right_sector[sec * left_size.shape[0] + q]])
    return mask, jnp.where(mask, vector[kind].astype(F32), 0.0)


def load_vectors(vectors, vector, sem):
    start_all([pltpu.make_async_copy(vectors.at[own_sector(kind)], vector.at[kind], sem) for kind in range(2)])


def first_kernel(left_size, right_size, right_sector, vectors, *rest):
    *blocks, out, vector, sem = rest
    half = len(MOVES) + 1
    lefts, rights = blocks[: half - 1], blocks[half:-1]
    load_vectors(vectors, vector, sem)
    for kind in range(2):
        _, start = start_vector(kind, left_size, right_size, right_sector, vector)
        out[kind] = apply(start.astype(BF16), kind, lefts, blocks[half - 1], rights, blocks[-1]).astype(BF16)


def second_kernel(left_size, right_size, right_sector, vectors, image_here, image_there, *rest):
    *blocks, out, vector, sem = rest
    half = len(MOVES) + 1
    lefts, rights = blocks[: half - 1], blocks[half:-1]
    width = vector.shape[1]
    upper = lax.axis_index("mpo") // 2 >= lax.axis_size("mpo") // 4
    load_vectors(vectors, vector, sem)
    parts = out.shape[0]
    rows = width // parts
    lane = lax.broadcasted_iota(jnp.int32, (8, width), 1)
    line = jnp.zeros((8, width), F32)
    rests = []
    for kind in range(2):
        mask, start = start_vector(kind, left_size, right_size, right_sector, vector)
        norm = total(start * start)
        scale = 1.0 / jnp.sqrt(norm / float(width * width) + 1e-06)
        image = jnp.where(mask, image_here[kind].astype(F32) + image_there[kind].astype(F32), 0.0) * scale
        unit = start * scale
        length = total(unit * unit)
        overlap = total(unit * image)
        ratio = jnp.where(length > 0.0, overlap / jnp.where(length > 0.0, length, 1.0), 0.0)
        rest = image - ratio * unit
        after = jnp.where(mask, apply(rest.astype(BF16), kind, lefts, blocks[half - 1], rights, blocks[-1]), 0.0)
        share = jnp.where(upper == (kind == 1), 1.0, 0.0)
        numbers = (
            share * norm,
            share * overlap,
            share * ratio,
            share * total(rest * rest),
            total(rest * after),
            total(unit * after) + share * total(rest * image),
            share * total(rest * unit),
        )
        place = own_sector(kind) * LANES
        for j, number in enumerate(numbers):
            line = jnp.where(lane == place + j, number, line)
        rests.append(rest)
        for d in range(parts):
            out[d, (1 + kind) * rows : (2 + kind) * rows] = after[d * rows : (d + 1) * rows]
    chosen = jnp.where(upper, rests[1], rests[0])
    for d in range(parts):
        out[d, :rows] = chosen[d * rows : (d + 1) * rows]
        out[d, 3 * rows :] = line


def finish_kernel(left_size, right_size, right_sector, vectors, pieces, shared, next_out, rest_out, coef_out, vector, sem):
    blocks, rows, width = next_out.shape
    sec = lax.axis_index("sec")
    part = lax.axis_index("mpo")
    devices = shared.shape[0]
    groups = PAD // rows
    load = pltpu.make_async_copy(vectors.at[:, pl.ds(pl.multiple_of(part // groups * PAD, PAD), PAD)], vector, sem)
    load.start()
    entries = float(devices * blocks * width * width)
    cells = float(width * width)
    stats = shared[:, 0, :]
    line = shared[sec][:1]
    chips = lax.axis_size("mpo") // 2
    lane = lax.broadcasted_iota(jnp.int32, stats.shape, 1) % LANES

    def field(x, j):
        return x if j == 0 else pltpu.roll(x, x.shape[1] - j, 1)

    lead = lane == 0
    norm = jnp.where(lead, field(stats, 0), 0.0)
    overlap = field(stats, 1)
    ratio = field(stats, 2)
    gain = 1.0 / jnp.sqrt(total(norm) / entries + 1e-06)
    mean = jnp.where(lead, norm, 0.0) / cells + 1e-06
    weight = jnp.where(lead, (gain * gain) * mean, 0.0)
    length = norm / mean
    alpha = total(jnp.where(lead, weight * overlap, 0.0)) / entries
    delta = jnp.where(lead, ratio - alpha, 0.0)
    rest_total = total(jnp.where(lead, weight * (field(stats, 3) + delta * delta * length + 2.0 * delta * field(stats, 6)), 0.0))
    beta = jnp.sqrt(rest_total / entries + 1e-06)
    inner = field(stats, 4) + delta * field(stats, 5) + delta * delta * overlap
    alpha_next = total(jnp.where(lead, weight * inner, 0.0)) / entries / beta / beta
    for j, number in enumerate((alpha, beta, alpha_next)):
        coef_out[j] = number[0, 0]
    load.wait()
    for q in range(blocks):
        cut, kind, core = q // 4, q // 2 % 2, q % 2
        lower = 2 * ((cut + 1 + kind) % (chips // 2)) + core
        higher = lower + chips
        lane_one = lax.broadcasted_iota(jnp.int32, line.shape, 1)
        norm_q = jnp.sum(jnp.where(lane_one == q * LANES, line, 0.0), axis=1, keepdims=True)
        ratio_q = jnp.sum(jnp.where(lane_one == q * LANES + 2, line, 0.0), axis=1, keepdims=True)
        root = jnp.sqrt(norm_q / cells + 1e-06)
        scale = gain * root
        row = lax.broadcasted_iota(jnp.int32, (rows, width), 0) + part * rows
        col = lax.broadcasted_iota(jnp.int32, (rows, width), 1)
        mask = (row < left_size[q]) & (col < right_size[right_sector[sec * blocks + q]])
        group = vector[q].astype(F32)
        own_rows = group[:rows]
        for j in range(1, groups):
            own_rows = jnp.where(part % groups == j, group[j * rows : (j + 1) * rows], own_rows)
        unit = jnp.where(mask, own_rows, 0.0) / root
        rest = pieces[higher if kind else lower, :rows]
        after_rows = slice((1 + kind) * rows, (2 + kind) * rows)
        after = pieces[lower, after_rows] + pieces[higher, after_rows]
        shift = ratio_q - alpha
        second = (scale / beta) * (rest + shift * unit)
        image = (scale / beta) * (after + shift * (rest + ratio_q * unit))
        next_out[q] = second
        rest_out[q] = image - alpha_next * second - (beta * scale) * unit


def shards(
    wavefunction,
    left_size,
    right_size,
    right_sector,
    left_environment,
    right_environment,
    term_weights,
):
    blocks, width, _ = wavefunction.shape
    terms = left_environment.shape[0]
    devices = lax.axis_size("sec")
    layers = lax.axis_size("mpo")
    rows = width // layers
    anywhere = pl.BlockSpec(memory_space=pl.ANY)
    scalars = pl.BlockSpec(memory_space=pltpu.SMEM)
    vmem = pl.BlockSpec(memory_space=pltpu.VMEM)

    chips = layers // 2
    long = terms * width
    routes = [[(p, (p + 2 * move) % layers) for p in range(layers)] for move, _ in MOVES]
    counts = [2 * len(kinds) for _, kinds in MOVES]
    cores = [(p, p ^ 1) for p in range(layers)]
    with jax.named_scope("pack_right"):
        right_out = pl.pallas_call(
            pack_right_kernel,
            out_shape=jax.ShapeDtypeStruct((devices, SLOTS, terms, width, width), BF16),
            in_specs=[scalars, anywhere],
            out_specs=anywhere,
            scratch_shapes=[pltpu.VMEM(right_environment.shape, BF16), pltpu.SemaphoreType.DMA((2,))],
            compiler_params=pltpu.CompilerParams(vmem_limit_bytes=60 * MIB),
        )(right_sector, right_environment)
    with jax.named_scope("right_over_sec"):
        arrived = lax.all_to_all(right_out, "sec", 0, 0, tiled=True)
    with jax.named_scope("pack_left"):
        lefts = pl.pallas_call(
            pack_left_kernel,
            out_shape=[jax.ShapeDtypeStruct((count * long + PAD, width), BF16) for count in counts],
            in_specs=[scalars, anywhere],
            out_specs=[anywhere] * len(MOVES),
            scratch_shapes=[
                pltpu.VMEM(left_environment.shape, BF16),
                pltpu.VMEM((PAD, width), BF16),
                pltpu.SemaphoreType.DMA((2,)),
            ],
            compiler_params=pltpu.CompilerParams(vmem_limit_bytes=8 * MIB),
        )(term_weights, left_environment)
    with jax.named_scope("left_over_z"):
        lefts = [lefts[0]] + [lax.ppermute(left, "mpo", route) for left, route in zip(lefts[1:], routes[1:])]
    with jax.named_scope("left_over_core"):
        given = pl.pallas_call(
            collect_left_kernel,
            out_shape=jax.ShapeDtypeStruct((blocks // 2, long + PAD, width), BF16),
            in_specs=[anywhere] * len(MOVES),
            out_specs=anywhere,
            scratch_shapes=[pltpu.SemaphoreType.DMA],
            compiler_params=pltpu.CompilerParams(vmem_limit_bytes=4 * MIB),
        )(*lefts)
        lefts.append(lax.ppermute(given, "mpo", cores))
        arrived, *lefts = lax.optimization_barrier((arrived, *lefts))
    with jax.named_scope("order"):
        rights = pl.pallas_call(
            order_kernel,
            out_shape=[jax.ShapeDtypeStruct((count, terms, width, width), BF16) for count in [2, 2] + counts[1:]],
            in_specs=[scalars, anywhere],
            out_specs=[anywhere] * (len(MOVES) + 1),
            scratch_shapes=[
                pltpu.VMEM((blocks, terms, width, width), BF16),
                pltpu.SMEM((blocks,), jnp.int32),
                pltpu.SemaphoreType.DMA((blocks + 1,)),
            ],
            compiler_params=pltpu.CompilerParams(vmem_limit_bytes=40 * MIB),
        )(right_sector, arrived.reshape(devices * SLOTS, terms, width, width))
    with jax.named_scope("right_over_z"):
        stayed = [rights[0], lax.ppermute(rights[1], "mpo", cores)]
        rights = [lax.ppermute(right, "mpo", route) for right, route in zip(rights[2:], routes[1:])]
    with jax.named_scope("right_over_core"):
        given = pl.pallas_call(
            collect_right_kernel,
            out_shape=jax.ShapeDtypeStruct((blocks // 2 - 2, terms, width, width), BF16),
            in_specs=[anywhere] * (len(MOVES) - 1),
            out_specs=anywhere,
            scratch_shapes=[pltpu.SemaphoreType.DMA],
            compiler_params=pltpu.CompilerParams(vmem_limit_bytes=4 * MIB),
        )(*rights)
        rights = stayed + rights + [lax.ppermute(given, "mpo", cores)]
    with jax.named_scope("first_image"):
        image_here = pl.pallas_call(
            first_kernel,
            out_shape=jax.ShapeDtypeStruct((2, width, width), BF16),
            in_specs=[scalars, scalars, scalars, anywhere] + [vmem] * (2 * len(MOVES) + 3),
            out_specs=vmem,
            scratch_shapes=[pltpu.VMEM((2, width, width), BF16), pltpu.SemaphoreType.DMA],
            compiler_params=pltpu.CompilerParams(vmem_limit_bytes=16 * MIB),
        )(left_size, right_size, right_sector, wavefunction, *lefts, *rights)
    with jax.named_scope("swap_images"):
        image_there = lax.ppermute(image_here, "mpo", [(p, (p + chips) % layers) for p in range(layers)])
    with jax.named_scope("second_image"):
        pieces = pl.pallas_call(
            second_kernel,
            out_shape=jax.ShapeDtypeStruct((layers, 3 * rows + 8, width), F32),
            in_specs=[scalars, scalars, scalars, anywhere] + [vmem] * (2 * len(MOVES) + 5),
            out_specs=vmem,
            scratch_shapes=[pltpu.VMEM((2, width, width), BF16), pltpu.SemaphoreType.DMA],
            compiler_params=pltpu.CompilerParams(vmem_limit_bytes=16 * MIB),
        )(left_size, right_size, right_sector, wavefunction, image_here, image_there, *lefts, *rights)
    with jax.named_scope("rows_over_mpo"):
        pieces = lax.all_to_all(pieces, "mpo", 0, 0, tiled=True)
    with jax.named_scope("numbers_over_sec"):
        line = jnp.sum(pieces[:, 3 * rows :, :], axis=0)
        shared = lax.all_to_all(jnp.broadcast_to(line[None], (devices, 8, width)), "sec", 0, 0, tiled=True)
    with jax.named_scope("finish"):
        next_vector, residual, coefficients = pl.pallas_call(
            finish_kernel,
            out_shape=(
                jax.ShapeDtypeStruct((blocks, rows, width), F32),
                jax.ShapeDtypeStruct((blocks, rows, width), F32),
                jax.ShapeDtypeStruct((3,), F32),
            ),
            in_specs=[scalars, scalars, scalars, anywhere, vmem, vmem],
            out_specs=(vmem, vmem, scalars),
            scratch_shapes=[pltpu.VMEM((blocks, PAD, width), BF16), pltpu.SemaphoreType.DMA],
            compiler_params=pltpu.CompilerParams(vmem_limit_bytes=8 * MIB),
        )(left_size, right_size, right_sector, wavefunction, pieces, shared)
    return (next_vector, residual, coefficients)


def solution(mesh):
    placed = (
        P("sec", None, None),
        P("sec"),
        P(),
        P(),
        P("mpo", "sec", None, None),
        P("mpo", "sec", None, None),
        P("mpo"),
    )
    return jax.shard_map(
        shards,
        mesh=mesh,
        in_specs=placed,
        out_specs=(P("sec", "mpo", None), P("sec", "mpo", None), P()),
        check_vma=False,
    )
```

```python
import jax
import jax.numpy as jnp
from jax import lax
from jax.experimental import pallas as pl
from jax.experimental.pallas import tpu as pltpu
from jax.sharding import PartitionSpec as P

F32 = jnp.float32
BF16 = jnp.bfloat16
SLOTS = 2
PAD = 16
LANES = 8
MIB = 1024 * 1024


def sector_of(chip, core, kind, chips):
    cuts = chips // 2
    return ((chip + chips - 1 - kind) % cuts) * 4 + kind * 2 + core


MOVES = ((0, (0, 1)), (2, (1,)), (-2, (0,)), (1, (0, 1)), (-1, (0, 1)))


def targets(own, chips):
    chip, core = own // 2, own % 2
    return [
        [sector_of((chip + move + chips) % chips, (core + side) % 2, kind, chips) for side in range(2) for kind in kinds]
        for move, kinds in MOVES
    ]


def parts_of(kind):
    found = []
    base = 0
    for index, (_, kinds) in enumerate(MOVES):
        if kind in kinds:
            found.append((index, kinds.index(kind), base + kinds.index(kind)))
        base += len(kinds)
    return found


def start_all(copies):
    for copy in copies:
        copy.start()
    for copy in copies:
        copy.wait()


def pack_right_kernel(right_sector, right_env, right_out, stage, sem):
    blocks = right_env.shape[1]
    devices = right_out.shape[0]
    sec = lax.axis_index("sec")
    load = pltpu.make_async_copy(right_env, stage, sem.at[0])
    load.start()
    base = sec * blocks
    picks = []
    copies = []
    for t in range(devices):
        first = jnp.int32(blocks * blocks)
        last = jnp.int32(0)
        for i in range(blocks):
            offset = right_sector[t * blocks + i] - base
            match = (offset >= 0) & (offset < blocks)
            first = jnp.where(match, jnp.minimum(first, offset + i * blocks), first)
            last = jnp.where(match, offset, last)
        picks.append((first & (blocks - 1), last))
        if t < devices // 4:
            continue
        if t == devices // 4:
            load.wait()
        for ready in range(t + 1 if t == devices // 4 else 1):
            target = ready if t == devices // 4 else t
            for k in range(SLOTS):
                copies.append(pltpu.make_async_copy(stage.at[:, picks[target][k]], right_out.at[target, k], sem.at[1]))
                copies[-1].start()
    for copy in copies:
        copy.wait()


def pack_left_kernel(weights, right_sector, left_env, *rest):
    *lefts, places, stage, wbuf, sem = rest
    terms, blocks, width, _ = left_env.shape
    sec = lax.axis_index("sec")
    own = lax.axis_index("mpo")
    load = pltpu.make_async_copy(left_env, stage, sem.at[0])
    load.start()
    row = lax.broadcasted_iota(jnp.int32, wbuf.shape, 0)
    vals = jnp.zeros(wbuf.shape, F32)
    for w in range(terms):
        whole = jnp.full(wbuf.shape, weights[w], F32)
        high = whole.astype(BF16).astype(F32)
        mid = (whole - high).astype(BF16).astype(F32)
        low = whole - high - mid
        for j, part in enumerate((high, mid, low)):
            vals = jnp.where(row == w * 3 + j, part, vals)
    wbuf[...] = vals.astype(BF16)
    load.wait()
    copies = []
    for left, sectors in zip(lefts, targets(own, lax.axis_size("mpo") // 2)):
        for place, q in enumerate(sectors):
            for w in range(terms):
                rows = pl.ds((place * terms + w) * width, width)
                copies.append(pltpu.make_async_copy(stage.at[w, q], left.at[rows], sem.at[1]))
        copies.append(pltpu.make_async_copy(wbuf, left.at[pl.ds(len(sectors) * terms * width, PAD)], sem.at[1]))
    for copy in copies:
        copy.start()
    shift = blocks.bit_length() - 1
    sources = [lax.shift_right_logical(right_sector[sec * blocks + q], shift) for q in range(blocks)]
    for q in range(blocks):
        again = jnp.bool_(False)
        for other in range(q):
            again = again | (sources[other] == sources[q])
        places[q] = sources[q] * SLOTS + jnp.where(again, 1, 0)
    for copy in copies:
        copy.wait()


def collect_left_kernel(*refs):
    *lefts, kept, given, sem = refs
    size = given.shape[1] - PAD
    copies = []
    place = 0
    for left, (_, kinds) in zip(lefts, MOVES):
        count = len(kinds)
        for j in range(count):
            for target, first in ((kept, j), (given, count + j)):
                for start, rows in ((first * size, pl.ds(0, size)), (2 * count * size, pl.ds(size, PAD))):
                    source = left.at[pl.ds(start, rows.size)]
                    copies.append(pltpu.make_async_copy(source, target.at[place, rows], sem))
            place += 1
    start_all(copies)


def collect_right_kernel(*refs):
    *rights, given, sem = refs
    copies = []
    place = 0
    for right, (_, kinds) in zip(rights, MOVES[1:]):
        count = len(kinds)
        copies.append(pltpu.make_async_copy(right.at[pl.ds(count, count)], given.at[pl.ds(place, count)], sem))
        place += count
    start_all(copies)


def order_kernel(places, arrived, *rest):
    *rights, sem = rest
    sectors = [q for group in targets(lax.axis_index("mpo"), lax.axis_size("mpo") // 2) for q in group]
    copies = []
    for right in rights:
        for place in range(right.shape[0]):
            copies.append(pltpu.make_async_copy(arrived.at[places[sectors[len(copies)]]], right.at[place], sem))
            copies[-1].start()
    for copy in copies:
        copy.wait()


def live(rows, left, right):
    row = lax.broadcasted_iota(jnp.int32, rows, 0)
    col = lax.broadcasted_iota(jnp.int32, rows, 1)
    return (row < left) & (col < right)


def total(x):
    return jnp.sum(jnp.sum(x, axis=0, keepdims=True), axis=1, keepdims=True)


def apply(block, kind, lefts, rights):
    _, terms, width, _ = rights[-1].shape
    size = terms * width
    acc = jnp.zeros((width, width), F32)
    for index, place, other in parts_of(kind):
        for side in range(2):
            left = lefts[side][other, :size]
            scale = lefts[side][other, size:].astype(F32)
            if index == 0:
                right = [rights[side][place, w] for w in range(terms)]
            elif side == 0:
                right = [rights[1 + index][place, w] for w in range(terms)]
            else:
                right = [rights[-1][other - 2, w] for w in range(terms)]
            half = jnp.dot(left, block, preferred_element_type=F32)
            halves = []
            for w in range(terms):
                weight = scale[3 * w : 3 * w + 1] + scale[3 * w + 1 : 3 * w + 2] + scale[3 * w + 2 : 3 * w + 3]
                halves.append((weight * half[w * width : (w + 1) * width]).astype(BF16))
            acc = acc + lax.dot_general(
                jnp.concatenate(halves, axis=1),
                jnp.concatenate(right, axis=1),
                (((1,), (1,)), ((), ())),
                preferred_element_type=F32,
            )
    return acc


def own_sector(kind):
    own = lax.axis_index("mpo")
    return sector_of(own // 2, own % 2, kind, lax.axis_size("mpo") // 2)


def start_vector(kind, left_size, right_size, right_sector, vector):
    width = vector.shape[1]
    q = own_sector(kind)
    sec = lax.axis_index("sec")
    mask = live((width, width), left_size[q], right_size[right_sector[sec * left_size.shape[0] + q]])
    return mask, jnp.where(mask, vector[kind].astype(F32), 0.0)


def load_vectors(vectors, vector, sem):
    start_all([pltpu.make_async_copy(vectors.at[own_sector(kind)], vector.at[kind], sem) for kind in range(2)])


def first_kernel(left_size, right_size, right_sector, vectors, *rest):
    *blocks, out, vector, sem = rest
    load_vectors(vectors, vector, sem)
    for kind in range(2):
        _, start = start_vector(kind, left_size, right_size, right_sector, vector)
        out[kind] = apply(start.astype(BF16), kind, blocks[:2], blocks[2:]).astype(BF16)


def second_kernel(left_size, right_size, right_sector, vectors, image_here, image_there, *rest):
    *blocks, out, vector, sem = rest
    width = vector.shape[1]
    upper = lax.axis_index("mpo") // 2 >= lax.axis_size("mpo") // 4
    load_vectors(vectors, vector, sem)
    parts = out.shape[0]
    rows = width // parts
    lane = lax.broadcasted_iota(jnp.int32, (8, width), 1)
    line = jnp.zeros((8, width), F32)
    rests = []
    for kind in range(2):
        mask, start = start_vector(kind, left_size, right_size, right_sector, vector)
        norm = total(start * start)
        scale = 1.0 / jnp.sqrt(norm / float(width * width) + 1e-06)
        image = jnp.where(mask, image_here[kind].astype(F32) + image_there[kind].astype(F32), 0.0) * scale
        unit = start * scale
        length = total(unit * unit)
        overlap = total(unit * image)
        ratio = jnp.where(length > 0.0, overlap / jnp.where(length > 0.0, length, 1.0), 0.0)
        rest = image - ratio * unit
        after = jnp.where(mask, apply(rest.astype(BF16), kind, blocks[:2], blocks[2:]), 0.0)
        share = jnp.where(upper == (kind == 1), 1.0, 0.0)
        numbers = (
            share * norm,
            share * overlap,
            share * ratio,
            share * total(rest * rest),
            total(rest * after),
            total(unit * after) + share * total(rest * image),
            share * total(rest * unit),
        )
        place = own_sector(kind) * LANES
        for j, number in enumerate(numbers):
            line = jnp.where(lane == place + j, number, line)
        rests.append(rest)
        for d in range(parts):
            out[d, (1 + kind) * rows : (2 + kind) * rows] = after[d * rows : (d + 1) * rows]
    chosen = jnp.where(upper, rests[1], rests[0])
    for d in range(parts):
        out[d, :rows] = chosen[d * rows : (d + 1) * rows]
        out[d, 3 * rows :] = line


def finish_kernel(left_size, right_size, right_sector, vectors, pieces, shared, next_out, rest_out, coef_out, vector, sem):
    blocks, rows, width = next_out.shape
    sec = lax.axis_index("sec")
    part = lax.axis_index("mpo")
    devices = shared.shape[0]
    groups = PAD // rows
    load = pltpu.make_async_copy(vectors.at[:, pl.ds(pl.multiple_of(part // groups * PAD, PAD), PAD)], vector, sem)
    load.start()
    entries = float(devices * blocks * width * width)
    cells = float(width * width)
    stats = shared[:, 0, :]
    line = shared[sec][:1]
    chips = lax.axis_size("mpo") // 2
    lane = lax.broadcasted_iota(jnp.int32, stats.shape, 1) % LANES

    def field(x, j):
        return x if j == 0 else pltpu.roll(x, x.shape[1] - j, 1)

    lead = lane == 0
    norm = jnp.where(lead, field(stats, 0), 0.0)
    overlap = field(stats, 1)
    ratio = field(stats, 2)
    gain = 1.0 / jnp.sqrt(total(norm) / entries + 1e-06)
    mean = jnp.where(lead, norm, 0.0) / cells + 1e-06
    weight = jnp.where(lead, (gain * gain) * mean, 0.0)
    length = norm / mean
    alpha = total(jnp.where(lead, weight * overlap, 0.0)) / entries
    delta = jnp.where(lead, ratio - alpha, 0.0)
    rest_total = total(jnp.where(lead, weight * (field(stats, 3) + delta * delta * length + 2.0 * delta * field(stats, 6)), 0.0))
    beta = jnp.sqrt(rest_total / entries + 1e-06)
    inner = field(stats, 4) + delta * field(stats, 5) + delta * delta * overlap
    alpha_next = total(jnp.where(lead, weight * inner, 0.0)) / entries / beta / beta
    for j, number in enumerate((alpha, beta, alpha_next)):
        coef_out[j] = number[0, 0]
    load.wait()
    for q in range(blocks):
        cut, kind, core = q // 4, q // 2 % 2, q % 2
        lower = 2 * ((cut + 1 + kind) % (chips // 2)) + core
        higher = lower + chips
        lane_one = lax.broadcasted_iota(jnp.int32, line.shape, 1)
        norm_q = jnp.sum(jnp.where(lane_one == q * LANES, line, 0.0), axis=1, keepdims=True)
        ratio_q = jnp.sum(jnp.where(lane_one == q * LANES + 2, line, 0.0), axis=1, keepdims=True)
        root = jnp.sqrt(norm_q / cells + 1e-06)
        scale = gain * root
        row = lax.broadcasted_iota(jnp.int32, (rows, width), 0) + part * rows
        col = lax.broadcasted_iota(jnp.int32, (rows, width), 1)
        mask = (row < left_size[q]) & (col < right_size[right_sector[sec * blocks + q]])
        group = vector[q].astype(F32)
        own_rows = group[:rows]
        for j in range(1, groups):
            own_rows = jnp.where(part % groups == j, group[j * rows : (j + 1) * rows], own_rows)
        unit = jnp.where(mask, own_rows, 0.0) / root
        rest = pieces[higher if kind else lower, :rows]
        after_rows = slice((1 + kind) * rows, (2 + kind) * rows)
        after = pieces[lower, after_rows] + pieces[higher, after_rows]
        shift = ratio_q - alpha
        second = (scale / beta) * (rest + shift * unit)
        image = (scale / beta) * (after + shift * (rest + ratio_q * unit))
        next_out[q] = second
        rest_out[q] = image - alpha_next * second - (beta * scale) * unit


def shards(
    wavefunction,
    left_size,
    right_size,
    right_sector,
    left_environment,
    right_environment,
    term_weights,
):
    blocks, width, _ = wavefunction.shape
    terms = left_environment.shape[0]
    devices = lax.axis_size("sec")
    layers = lax.axis_size("mpo")
    rows = width // layers
    anywhere = pl.BlockSpec(memory_space=pl.ANY)
    scalars = pl.BlockSpec(memory_space=pltpu.SMEM)
    vmem = pl.BlockSpec(memory_space=pltpu.VMEM)

    chips = layers // 2
    long = terms * width
    routes = [[(p, (p + 2 * move) % layers) for p in range(layers)] for move, _ in MOVES]
    counts = [2 * len(kinds) for _, kinds in MOVES]
    cores = [(p, p ^ 1) for p in range(layers)]
    with jax.named_scope("pack_right"):
        right_out = pl.pallas_call(
            pack_right_kernel,
            out_shape=jax.ShapeDtypeStruct((devices, SLOTS, terms, width, width), BF16),
            in_specs=[scalars, anywhere],
            out_specs=anywhere,
            scratch_shapes=[pltpu.VMEM(right_environment.shape, BF16), pltpu.SemaphoreType.DMA((2,))],
            compiler_params=pltpu.CompilerParams(vmem_limit_bytes=60 * MIB),
        )(right_sector, right_environment)
    with jax.named_scope("right_over_sec"):
        arrived = lax.all_to_all(right_out, "sec", 0, 0, tiled=True)
    with jax.named_scope("pack_left"):
        *lefts, places = pl.pallas_call(
            pack_left_kernel,
            out_shape=[jax.ShapeDtypeStruct((count * long + PAD, width), BF16) for count in counts]
            + [jax.ShapeDtypeStruct((blocks,), jnp.int32)],
            in_specs=[scalars, scalars, anywhere],
            out_specs=[anywhere] * len(MOVES) + [scalars],
            scratch_shapes=[
                pltpu.VMEM(left_environment.shape, BF16),
                pltpu.VMEM((PAD, width), BF16),
                pltpu.SemaphoreType.DMA((2,)),
            ],
            compiler_params=pltpu.CompilerParams(vmem_limit_bytes=8 * MIB),
        )(term_weights, right_sector, left_environment)
    with jax.named_scope("left_over_z"):
        lefts = [lefts[0]] + [lax.ppermute(left, "mpo", route) for left, route in zip(lefts[1:], routes[1:])]
    with jax.named_scope("left_over_core"):
        kept, given = pl.pallas_call(
            collect_left_kernel,
            out_shape=(jax.ShapeDtypeStruct((blocks // 2, long + PAD, width), BF16),) * 2,
            in_specs=[anywhere] * len(MOVES),
            out_specs=(anywhere, anywhere),
            scratch_shapes=[pltpu.SemaphoreType.DMA],
            compiler_params=pltpu.CompilerParams(vmem_limit_bytes=4 * MIB),
        )(*lefts)
        lefts = [kept, lax.ppermute(given, "mpo", cores)]
        arrived, *lefts = lax.optimization_barrier((arrived, *lefts))
    with jax.named_scope("order"):
        rights = pl.pallas_call(
            order_kernel,
            out_shape=[jax.ShapeDtypeStruct((count, terms, width, width), BF16) for count in [2, 2] + counts[1:]],
            in_specs=[scalars, anywhere],
            out_specs=[anywhere] * (len(MOVES) + 1),
            scratch_shapes=[pltpu.SemaphoreType.DMA],
            compiler_params=pltpu.CompilerParams(vmem_limit_bytes=4 * MIB),
        )(places, arrived.reshape(devices * SLOTS, terms, width, width))
    with jax.named_scope("right_over_z"):
        stayed = [rights[0], lax.ppermute(rights[1], "mpo", cores)]
        rights = [lax.ppermute(right, "mpo", route) for right, route in zip(rights[2:], routes[1:])]
    with jax.named_scope("right_over_core"):
        given = pl.pallas_call(
            collect_right_kernel,
            out_shape=jax.ShapeDtypeStruct((blocks // 2 - 2, terms, width, width), BF16),
            in_specs=[anywhere] * (len(MOVES) - 1),
            out_specs=anywhere,
            scratch_shapes=[pltpu.SemaphoreType.DMA],
            compiler_params=pltpu.CompilerParams(vmem_limit_bytes=4 * MIB),
        )(*rights)
        rights = stayed + rights + [lax.ppermute(given, "mpo", cores)]
    with jax.named_scope("first_image"):
        image_here = pl.pallas_call(
            first_kernel,
            out_shape=jax.ShapeDtypeStruct((2, width, width), BF16),
            in_specs=[scalars, scalars, scalars, anywhere] + [vmem] * (len(MOVES) + 4),
            out_specs=vmem,
            scratch_shapes=[pltpu.VMEM((2, width, width), BF16), pltpu.SemaphoreType.DMA],
            compiler_params=pltpu.CompilerParams(vmem_limit_bytes=16 * MIB),
        )(left_size, right_size, right_sector, wavefunction, *lefts, *rights)
    with jax.named_scope("swap_images"):
        image_there = lax.ppermute(image_here, "mpo", [(p, (p + chips) % layers) for p in range(layers)])
    with jax.named_scope("second_image"):
        pieces = pl.pallas_call(
            second_kernel,
            out_shape=jax.ShapeDtypeStruct((layers, 3 * rows + 8, width), F32),
            in_specs=[scalars, scalars, scalars, anywhere] + [vmem] * (len(MOVES) + 6),
            out_specs=vmem,
            scratch_shapes=[pltpu.VMEM((2, width, width), BF16), pltpu.SemaphoreType.DMA],
            compiler_params=pltpu.CompilerParams(vmem_limit_bytes=16 * MIB),
        )(left_size, right_size, right_sector, wavefunction, image_here, image_there, *lefts, *rights)
    with jax.named_scope("rows_over_mpo"):
        pieces = lax.all_to_all(pieces, "mpo", 0, 0, tiled=True)
    with jax.named_scope("numbers_over_sec"):
        line = jnp.sum(pieces[:, 3 * rows :, :], axis=0)
        shared = lax.all_to_all(jnp.broadcast_to(line[None], (devices, 8, width)), "sec", 0, 0, tiled=True)
    with jax.named_scope("finish"):
        next_vector, residual, coefficients = pl.pallas_call(
            finish_kernel,
            out_shape=(
                jax.ShapeDtypeStruct((blocks, rows, width), F32),
                jax.ShapeDtypeStruct((blocks, rows, width), F32),
                jax.ShapeDtypeStruct((3,), F32),
            ),
            in_specs=[scalars, scalars, scalars, anywhere, vmem, vmem],
            out_specs=(vmem, vmem, scalars),
            scratch_shapes=[pltpu.VMEM((blocks, PAD, width), BF16), pltpu.SemaphoreType.DMA],
            compiler_params=pltpu.CompilerParams(vmem_limit_bytes=8 * MIB),
        )(left_size, right_size, right_sector, wavefunction, pieces, shared)
    return (next_vector, residual, coefficients)


def solution(mesh):
    placed = (
        P("sec", None, None),
        P("sec"),
        P(),
        P(),
        P("mpo", "sec", None, None),
        P("mpo", "sec", None, None),
        P("mpo"),
    )
    return jax.shard_map(
        shards,
        mesh=mesh,
        in_specs=placed,
        out_specs=(P("sec", "mpo", None), P("sec", "mpo", None), P()),
        check_vma=False,
    )
```

```python
import jax
import jax.numpy as jnp
from jax import lax
from jax.experimental import pallas as pl
from jax.experimental.pallas import tpu as pltpu
from jax.sharding import PartitionSpec as P

F32 = jnp.float32
BF16 = jnp.bfloat16
SLOTS = 2
PAD = 16
LANES = 8
MIB = 1024 * 1024


def sector_of(chip, core, kind, chips):
    cuts = chips // 2
    return ((chip + chips - 1 - kind) % cuts) * 4 + kind * 2 + core


MOVES = ((0, (0, 1)), (2, (1,)), (-2, (0,)), (1, (0, 1)), (-1, (0, 1)))


def targets(own, chips):
    chip, core = own // 2, own % 2
    return [
        [sector_of((chip + move + chips) % chips, (core + side) % 2, kind, chips) for side in range(2) for kind in kinds]
        for move, kinds in MOVES
    ]


def parts_of(kind):
    found = []
    base = 0
    for index, (_, kinds) in enumerate(MOVES):
        if kind in kinds:
            found.append((index, kinds.index(kind), base + kinds.index(kind)))
        base += len(kinds)
    return found


def start_all(copies):
    for copy in copies:
        copy.start()
    for copy in copies:
        copy.wait()


def pack_right_kernel(right_sector, right_env, right_out, stage, sem):
    blocks = right_env.shape[1]
    devices = right_out.shape[0]
    sec = lax.axis_index("sec")
    load = pltpu.make_async_copy(right_env, stage, sem.at[0])
    load.start()
    base = sec * blocks
    picks = []
    copies = []
    for t in range(devices):
        first = jnp.int32(blocks * blocks)
        last = jnp.int32(0)
        for i in range(blocks):
            offset = right_sector[t * blocks + i] - base
            match = (offset >= 0) & (offset < blocks)
            first = jnp.where(match, jnp.minimum(first, offset + i * blocks), first)
            last = jnp.where(match, offset, last)
        picks.append((first & (blocks - 1), last))
        if t < devices // 4:
            continue
        if t == devices // 4:
            load.wait()
        for ready in range(t + 1 if t == devices // 4 else 1):
            target = ready if t == devices // 4 else t
            for k in range(SLOTS):
                copies.append(pltpu.make_async_copy(stage.at[:, picks[target][k]], right_out.at[target, k], sem.at[1]))
                copies[-1].start()
    for copy in copies:
        copy.wait()


def pack_left_kernel(weights, right_sector, left_env, *rest):
    *lefts, places, stage, wbuf, sem = rest
    terms, blocks, width, _ = left_env.shape
    sec = lax.axis_index("sec")
    own = lax.axis_index("mpo")
    load = pltpu.make_async_copy(left_env, stage, sem.at[0])
    load.start()
    row = lax.broadcasted_iota(jnp.int32, wbuf.shape, 0)
    vals = jnp.zeros(wbuf.shape, F32)
    for w in range(terms):
        whole = jnp.full(wbuf.shape, weights[w], F32)
        high = whole.astype(BF16).astype(F32)
        mid = (whole - high).astype(BF16).astype(F32)
        low = whole - high - mid
        for j, part in enumerate((high, mid, low)):
            vals = jnp.where(row == w * 3 + j, part, vals)
    wbuf[...] = vals.astype(BF16)
    load.wait()
    copies = []
    for left, sectors in zip(lefts, targets(own, lax.axis_size("mpo") // 2)):
        for place, q in enumerate(sectors):
            for w in range(terms):
                rows = pl.ds((place * terms + w) * width, width)
                copies.append(pltpu.make_async_copy(stage.at[w, q], left.at[rows], sem.at[1]))
        copies.append(pltpu.make_async_copy(wbuf, left.at[pl.ds(len(sectors) * terms * width, PAD)], sem.at[1]))
    for copy in copies:
        copy.start()
    shift = blocks.bit_length() - 1
    sources = [lax.shift_right_logical(right_sector[sec * blocks + q], shift) for q in range(blocks)]
    for q in range(blocks):
        again = jnp.bool_(False)
        for other in range(q):
            again = again | (sources[other] == sources[q])
        places[q] = sources[q] * SLOTS + jnp.where(again, 1, 0)
    for copy in copies:
        copy.wait()


def collect_left_kernel(*refs):
    *lefts, kept, given, sem = refs
    size = given.shape[1] - PAD
    copies = []
    place = 0
    for left, (_, kinds) in zip(lefts, MOVES):
        count = len(kinds)
        for j in range(count):
            for target, first in ((kept, j), (given, count + j)):
                for start, rows in ((first * size, pl.ds(0, size)), (2 * count * size, pl.ds(size, PAD))):
                    source = left.at[pl.ds(start, rows.size)]
                    copies.append(pltpu.make_async_copy(source, target.at[place, rows], sem))
            place += 1
    start_all(copies)


def collect_right_kernel(*refs):
    *rights, given, sem = refs
    copies = []
    place = 0
    for right, (_, kinds) in zip(rights, MOVES[1:]):
        count = len(kinds)
        copies.append(pltpu.make_async_copy(right.at[pl.ds(count, count)], given.at[pl.ds(place, count)], sem))
        place += count
    start_all(copies)


def order_kernel(places, arrived, *rest):
    *rights, sem = rest
    sectors = [q for group in targets(lax.axis_index("mpo"), lax.axis_size("mpo") // 2) for q in group]
    copies = []
    for right in rights:
        for place in range(right.shape[0]):
            copies.append(pltpu.make_async_copy(arrived.at[places[sectors[len(copies)]]], right.at[place], sem))
            copies[-1].start()
    for copy in copies:
        copy.wait()


def live(rows, left, right):
    row = lax.broadcasted_iota(jnp.int32, rows, 0)
    col = lax.broadcasted_iota(jnp.int32, rows, 1)
    return (row < left) & (col < right)


def total(x):
    return jnp.sum(jnp.sum(x, axis=0, keepdims=True), axis=1, keepdims=True)


def split(x):
    high = x.astype(BF16)
    return high, (x - high.astype(F32)).astype(BF16)


def apply(block, kind, lefts, rights):
    _, terms, width, _ = rights[-1].shape
    size = terms * width
    acc = jnp.zeros((width, width), F32)
    for index, place, other in parts_of(kind):
        for side in range(2):
            left = lefts[side][other, :size]
            scale = lefts[side][other, size:].astype(F32)
            if index == 0:
                right = [rights[side][place, w] for w in range(terms)]
            elif side == 0:
                right = [rights[1 + index][place, w] for w in range(terms)]
            else:
                right = [rights[-1][other - 2, w] for w in range(terms)]
            half = jnp.dot(left, block, preferred_element_type=F32)
            if block.shape[1] > width:
                half = half[:, :width] + half[:, width:]
            halves = []
            for w in range(terms):
                weight = scale[3 * w : 3 * w + 1] + scale[3 * w + 1 : 3 * w + 2] + scale[3 * w + 2 : 3 * w + 3]
                halves.append(split(weight * half[w * width : (w + 1) * width]))
            both = lax.dot_general(
                jnp.concatenate([jnp.concatenate(part, axis=1) for part in zip(*halves)], axis=0),
                jnp.concatenate(right, axis=1),
                (((1,), (1,)), ((), ())),
                preferred_element_type=F32,
            )
            acc = acc + (both[:width] + both[width:])
    return acc


def own_sector(kind):
    own = lax.axis_index("mpo")
    return sector_of(own // 2, own % 2, kind, lax.axis_size("mpo") // 2)


def start_vector(kind, left_size, right_size, right_sector, vector):
    width = vector.shape[1]
    q = own_sector(kind)
    sec = lax.axis_index("sec")
    mask = live((width, width), left_size[q], right_size[right_sector[sec * left_size.shape[0] + q]])
    return mask, jnp.where(mask, vector[kind].astype(F32), 0.0)


def load_vectors(vectors, vector, sem):
    start_all([pltpu.make_async_copy(vectors.at[own_sector(kind)], vector.at[kind], sem) for kind in range(2)])


def scaled(start):
    cells = float(start.shape[0] * start.shape[1])
    norm = total(start * start)
    unit = start * (1.0 / jnp.sqrt(norm / cells + 1e-06))
    return norm, unit, total(unit * unit)


def over(top, bottom):
    return jnp.where(bottom > 0.0, top / jnp.where(bottom > 0.0, bottom, 1.0), 0.0)


def first_kernel(left_size, right_size, right_sector, vectors, *rest):
    *blocks, out, ratios, vector, sem = rest
    load_vectors(vectors, vector, sem)
    row = lax.broadcasted_iota(jnp.int32, ratios.shape, 0)
    found = jnp.zeros(ratios.shape, F32)
    for kind in range(2):
        mask, start = start_vector(kind, left_size, right_size, right_sector, vector)
        norm, unit, length = scaled(start)
        scale = 1.0 / jnp.sqrt(norm / float(start.shape[0] * start.shape[1]) + 1e-06)
        image = jnp.where(mask, apply(start.astype(BF16), kind, blocks[:2], blocks[2:]), 0.0) * scale
        ratio = over(total(unit * image), length)
        out[kind] = (image - ratio * unit).astype(BF16)
        found = jnp.where(row == kind, ratio, found)
    ratios[...] = found


def second_kernel(left_size, right_size, right_sector, vectors, ratios, image_here, image_there, *rest):
    *blocks, out, vector, sem = rest
    width = vector.shape[1]
    upper = lax.axis_index("mpo") // 2 >= lax.axis_size("mpo") // 4
    load_vectors(vectors, vector, sem)
    parts = out.shape[0]
    rows = width // parts
    lane = lax.broadcasted_iota(jnp.int32, (8, width), 1)
    line = jnp.zeros((8, width), F32)
    rests = []
    afters = []
    for kind in range(2):
        mask, start = start_vector(kind, left_size, right_size, right_sector, vector)
        norm, unit, length = scaled(start)
        rest = image_here[kind].astype(F32) + image_there[kind].astype(F32)
        block = jnp.concatenate(split(rest), axis=1)
        after = jnp.where(mask, apply(block, kind, blocks[:2], blocks[2:]), 0.0)
        square = total(rest * rest)
        on_rest = total(rest * after)
        on_unit = total(unit * after)
        rest_ratio = over(on_rest, square)
        unit_ratio = over(on_unit, length)
        share = jnp.where(upper == (kind == 1), 1.0, 0.0)
        numbers = (
            share * norm,
            ratios[kind : kind + 1, :1],
            share * square,
            on_rest,
            on_unit,
            share * total(rest * unit),
            rest_ratio,
            unit_ratio,
        )
        after = after - rest_ratio * rest - unit_ratio * unit
        place = own_sector(kind) * LANES
        for j, number in enumerate(numbers):
            line = jnp.where(lane == place + j, number, line)
        rests.append(rest)
        afters.append(after)
    chosen = jnp.where(upper, rests[1], rests[0])
    high, _ = split(line)
    mid, low = split(line - high.astype(F32))
    row = lax.broadcasted_iota(jnp.int32, line.shape, 0)
    coded = jnp.where(row == 0, high.astype(F32), jnp.where(row == 1, mid.astype(F32), jnp.where(row == 2, low.astype(F32), 0.0)))
    for d in range(parts):
        own_rows = [x[d * rows : (d + 1) * rows] for x in (chosen, *afters)]
        out[d] = jnp.concatenate([*own_rows, coded], axis=0).astype(BF16)


def finish_kernel(left_size, right_size, right_sector, vectors, pieces, shared, next_out, rest_out, coef_out, vector, sem):
    blocks, rows, width = next_out.shape
    sec = lax.axis_index("sec")
    part = lax.axis_index("mpo")
    devices = shared.shape[0]
    groups = PAD // rows
    load = pltpu.make_async_copy(vectors.at[:, pl.ds(pl.multiple_of(part // groups * PAD, PAD), PAD)], vector, sem)
    load.start()
    entries = float(devices * blocks * width * width)
    cells = float(width * width)
    stats = shared[:, 0, :]
    line = shared[sec][:1]
    chips = lax.axis_size("mpo") // 2
    lane = lax.broadcasted_iota(jnp.int32, stats.shape, 1) % LANES

    def field(x, j):
        return x if j == 0 else pltpu.roll(x, x.shape[1] - j, 1)

    lead = lane == 0
    norm = jnp.where(lead, field(stats, 0), 0.0)
    ratio, square, on_rest, on_unit, skew = (field(stats, j) for j in range(1, 6))
    gain = 1.0 / jnp.sqrt(total(norm) / entries + 1e-06)
    mean = norm / cells + 1e-06
    weight = jnp.where(lead, (gain * gain) * mean, 0.0)
    length = norm / mean
    overlap = ratio * length + skew
    alpha = total(jnp.where(lead, weight * overlap, 0.0)) / entries
    delta = jnp.where(lead, ratio - alpha, 0.0)
    rest_total = total(jnp.where(lead, weight * (square + delta * delta * length + 2.0 * delta * skew), 0.0))
    beta = jnp.sqrt(rest_total / entries + 1e-06)
    inner = on_rest + delta * (on_unit + square + ratio * skew) + delta * delta * overlap
    alpha_next = total(jnp.where(lead, weight * inner, 0.0)) / entries / beta / beta
    for j, number in enumerate((alpha, beta, alpha_next)):
        coef_out[j] = number[0, 0]
    load.wait()
    for q in range(blocks):
        cut, kind, core = q // 4, q // 2 % 2, q % 2
        lower = 2 * ((cut + 1 + kind) % (chips // 2)) + core
        higher = lower + chips
        norm_q, ratio_q, rest_q, unit_q = (line[:, q * LANES + j : q * LANES + j + 1] for j in (0, 1, 6, 7))
        root = jnp.sqrt(norm_q / cells + 1e-06)
        scale = gain * root
        row = lax.broadcasted_iota(jnp.int32, (rows, width), 0) + part * rows
        col = lax.broadcasted_iota(jnp.int32, (rows, width), 1)
        mask = (row < left_size[q]) & (col < right_size[right_sector[sec * blocks + q]])
        group = vector[q].astype(F32)
        own_rows = group[:rows]
        for j in range(1, groups):
            own_rows = jnp.where(part % groups == j, group[j * rows : (j + 1) * rows], own_rows)
        unit = jnp.where(mask, own_rows, 0.0) / root
        sent = [pieces[owner].astype(F32) for owner in (lower, higher)]
        rest = sent[kind][:rows]
        after_rows = slice((1 + kind) * rows, (2 + kind) * rows)
        after = sent[0][after_rows] + sent[1][after_rows]
        shift = ratio_q - alpha
        second = (scale / beta) * (rest + shift * unit)
        next_out[q] = second
        on_second = rest_q + shift - alpha_next
        on_first = unit_q + shift * (ratio_q - alpha_next)
        rest_out[q] = (scale / beta) * (after + on_second * rest + on_first * unit) - (beta * scale) * unit


def shards(
    wavefunction,
    left_size,
    right_size,
    right_sector,
    left_environment,
    right_environment,
    term_weights,
):
    blocks, width, _ = wavefunction.shape
    terms = left_environment.shape[0]
    devices = lax.axis_size("sec")
    layers = lax.axis_size("mpo")
    rows = width // layers
    anywhere = pl.BlockSpec(memory_space=pl.ANY)
    scalars = pl.BlockSpec(memory_space=pltpu.SMEM)
    vmem = pl.BlockSpec(memory_space=pltpu.VMEM)

    chips = layers // 2
    long = terms * width
    routes = [[(p, (p + 2 * move) % layers) for p in range(layers)] for move, _ in MOVES]
    counts = [2 * len(kinds) for _, kinds in MOVES]
    cores = [(p, p ^ 1) for p in range(layers)]
    with jax.named_scope("pack_right"):
        right_out = pl.pallas_call(
            pack_right_kernel,
            out_shape=jax.ShapeDtypeStruct((devices, SLOTS, terms, width, width), BF16),
            in_specs=[scalars, anywhere],
            out_specs=anywhere,
            scratch_shapes=[pltpu.VMEM(right_environment.shape, BF16), pltpu.SemaphoreType.DMA((2,))],
            compiler_params=pltpu.CompilerParams(vmem_limit_bytes=60 * MIB),
        )(right_sector, right_environment)
    with jax.named_scope("right_over_sec"):
        arrived = lax.all_to_all(right_out, "sec", 0, 0, tiled=True)
    with jax.named_scope("pack_left"):
        *lefts, places = pl.pallas_call(
            pack_left_kernel,
            out_shape=[jax.ShapeDtypeStruct((count * long + PAD, width), BF16) for count in counts]
            + [jax.ShapeDtypeStruct((blocks,), jnp.int32)],
            in_specs=[scalars, scalars, anywhere],
            out_specs=[anywhere] * len(MOVES) + [scalars],
            scratch_shapes=[
                pltpu.VMEM(left_environment.shape, BF16),
                pltpu.VMEM((PAD, width), BF16),
                pltpu.SemaphoreType.DMA((2,)),
            ],
            compiler_params=pltpu.CompilerParams(vmem_limit_bytes=8 * MIB),
        )(term_weights, right_sector, left_environment)
    with jax.named_scope("left_over_z"):
        lefts = [lefts[0]] + [lax.ppermute(left, "mpo", route) for left, route in zip(lefts[1:], routes[1:])]
    with jax.named_scope("left_over_core"):
        kept, given = pl.pallas_call(
            collect_left_kernel,
            out_shape=(jax.ShapeDtypeStruct((blocks // 2, long + PAD, width), BF16),) * 2,
            in_specs=[anywhere] * len(MOVES),
            out_specs=(anywhere, anywhere),
            scratch_shapes=[pltpu.SemaphoreType.DMA],
            compiler_params=pltpu.CompilerParams(vmem_limit_bytes=4 * MIB),
        )(*lefts)
        lefts = [kept, lax.ppermute(given, "mpo", cores)]
        arrived, *lefts = lax.optimization_barrier((arrived, *lefts))
    with jax.named_scope("order"):
        rights = pl.pallas_call(
            order_kernel,
            out_shape=[jax.ShapeDtypeStruct((count, terms, width, width), BF16) for count in [2, 2] + counts[1:]],
            in_specs=[scalars, anywhere],
            out_specs=[anywhere] * (len(MOVES) + 1),
            scratch_shapes=[pltpu.SemaphoreType.DMA],
            compiler_params=pltpu.CompilerParams(vmem_limit_bytes=4 * MIB),
        )(places, arrived.reshape(devices * SLOTS, terms, width, width))
    with jax.named_scope("right_over_z"):
        stayed = [rights[0], lax.ppermute(rights[1], "mpo", cores)]
        rights = [lax.ppermute(right, "mpo", route) for right, route in zip(rights[2:], routes[1:])]
    with jax.named_scope("right_over_core"):
        given = pl.pallas_call(
            collect_right_kernel,
            out_shape=jax.ShapeDtypeStruct((blocks // 2 - 2, terms, width, width), BF16),
            in_specs=[anywhere] * (len(MOVES) - 1),
            out_specs=anywhere,
            scratch_shapes=[pltpu.SemaphoreType.DMA],
            compiler_params=pltpu.CompilerParams(vmem_limit_bytes=4 * MIB),
        )(*rights)
        rights = stayed + rights + [lax.ppermute(given, "mpo", cores)]
    with jax.named_scope("first_image"):
        image_here, ratios = pl.pallas_call(
            first_kernel,
            out_shape=(
                jax.ShapeDtypeStruct((2, width, width), BF16),
                jax.ShapeDtypeStruct((8, width), F32),
            ),
            in_specs=[scalars, scalars, scalars, anywhere] + [vmem] * (len(MOVES) + 4),
            out_specs=(vmem, vmem),
            scratch_shapes=[pltpu.VMEM((2, width, width), BF16), pltpu.SemaphoreType.DMA],
            compiler_params=pltpu.CompilerParams(vmem_limit_bytes=16 * MIB),
        )(left_size, right_size, right_sector, wavefunction, *lefts, *rights)
    with jax.named_scope("swap_images"):
        image_there = lax.ppermute(image_here, "mpo", [(p, (p + chips) % layers) for p in range(layers)])
    with jax.named_scope("second_image"):
        pieces = pl.pallas_call(
            second_kernel,
            out_shape=jax.ShapeDtypeStruct((layers, 3 * rows + 8, width), BF16),
            in_specs=[scalars, scalars, scalars, anywhere] + [vmem] * (len(MOVES) + 7),
            out_specs=vmem,
            scratch_shapes=[pltpu.VMEM((2, width, width), BF16), pltpu.SemaphoreType.DMA],
            compiler_params=pltpu.CompilerParams(vmem_limit_bytes=16 * MIB),
        )(left_size, right_size, right_sector, wavefunction, ratios, image_here, image_there, *lefts, *rights)
    with jax.named_scope("rows_over_mpo"):
        pieces = lax.all_to_all(pieces, "mpo", 0, 0, tiled=True)
    with jax.named_scope("numbers_over_sec"):
        line = jnp.sum(pieces[:, 3 * rows :, :].astype(F32), axis=(0, 1))
        shared = lax.all_to_all(jnp.broadcast_to(line[None, None], (devices, 8, width)), "sec", 0, 0, tiled=True)
    with jax.named_scope("finish"):
        next_vector, residual, coefficients = pl.pallas_call(
            finish_kernel,
            out_shape=(
                jax.ShapeDtypeStruct((blocks, rows, width), F32),
                jax.ShapeDtypeStruct((blocks, rows, width), F32),
                jax.ShapeDtypeStruct((3,), F32),
            ),
            in_specs=[scalars, scalars, scalars, anywhere, vmem, vmem],
            out_specs=(vmem, vmem, scalars),
            scratch_shapes=[pltpu.VMEM((blocks, PAD, width), BF16), pltpu.SemaphoreType.DMA],
            compiler_params=pltpu.CompilerParams(vmem_limit_bytes=8 * MIB),
        )(left_size, right_size, right_sector, wavefunction, pieces, shared)
    return (next_vector, residual, coefficients)


def solution(mesh):
    placed = (
        P("sec", None, None),
        P("sec"),
        P(),
        P(),
        P("mpo", "sec", None, None),
        P("mpo", "sec", None, None),
        P("mpo"),
    )
    return jax.shard_map(
        shards,
        mesh=mesh,
        in_specs=placed,
        out_specs=(P("sec", "mpo", None), P("sec", "mpo", None), P()),
        check_vma=False,
    )
```

```python
import jax
import jax.numpy as jnp
from jax import lax
from jax.experimental import pallas as pl
from jax.experimental.pallas import tpu as pltpu
from jax.sharding import PartitionSpec as P

F32 = jnp.float32
BF16 = jnp.bfloat16
SLOTS = 2
PAD = 16
LANES = 8
MIB = 1024 * 1024


def sector_of(chip, core, kind, chips):
    cuts = chips // 2
    return ((chip + chips - 1 - kind) % cuts) * 4 + kind * 2 + core


MOVES = ((0, (0, 1)), (2, (1,)), (-2, (0,)), (1, (0, 1)), (-1, (0, 1)))


def targets(own, chips):
    chip, core = own // 2, own % 2
    return [
        [sector_of((chip + move + chips) % chips, (core + side) % 2, kind, chips) for side in range(2) for kind in kinds]
        for move, kinds in MOVES
    ]


def parts_of(kind):
    found = []
    base = 0
    for index, (_, kinds) in enumerate(MOVES):
        if kind in kinds:
            found.append((index, kinds.index(kind), base + kinds.index(kind)))
        base += len(kinds)
    return found


def start_all(copies):
    for copy in copies:
        copy.start()
    for copy in copies:
        copy.wait()


def pack_right_kernel(right_sector, right_env, right_out, stage, sem):
    blocks = right_env.shape[1]
    devices = right_out.shape[0]
    sec = lax.axis_index("sec")
    load = pltpu.make_async_copy(right_env, stage, sem.at[0])
    load.start()
    base = sec * blocks
    picks = []
    copies = []
    seconds = []
    for t in range(devices):
        first = jnp.int32(blocks * blocks)
        last = jnp.int32(0)
        for i in range(blocks):
            offset = right_sector[t * blocks + i] - base
            match = (offset >= 0) & (offset < blocks)
            first = jnp.where(match, jnp.minimum(first, offset + i * blocks), first)
            last = jnp.where(match, offset, last)
        picks.append((first & (blocks - 1), last))
        if t < devices // 4:
            continue
        if t == devices // 4:
            load.wait()
        for ready in range(t + 1 if t == devices // 4 else 1):
            target = ready if t == devices // 4 else t
            first, last = picks[target]
            copy = pltpu.make_async_copy(stage.at[:, first], right_out.at[target, 0], sem.at[1])
            copy.start()
            copies.append(copy)
            copy = pltpu.make_async_copy(stage.at[:, last], right_out.at[target, 1], sem.at[2])
            pl.when(first != last)(copy.start)
            seconds.append((first != last, copy))
    for copy in copies:
        copy.wait()
    for there, copy in seconds:
        pl.when(there)(copy.wait)


def pack_left_kernel(weights, right_sector, left_env, *rest):
    *lefts, places, stage, wbuf, sem = rest
    terms, blocks, width, _ = left_env.shape
    sec = lax.axis_index("sec")
    own = lax.axis_index("mpo")
    load = pltpu.make_async_copy(left_env, stage, sem.at[0])
    load.start()
    row = lax.broadcasted_iota(jnp.int32, wbuf.shape, 0)
    vals = jnp.zeros(wbuf.shape, F32)
    for w in range(terms):
        whole = jnp.full(wbuf.shape, weights[w], F32)
        high = whole.astype(BF16).astype(F32)
        mid = (whole - high).astype(BF16).astype(F32)
        low = whole - high - mid
        for j, part in enumerate((high, mid, low)):
            vals = jnp.where(row == w * 3 + j, part, vals)
    wbuf[...] = vals.astype(BF16)
    load.wait()
    copies = []
    for left, sectors in zip(lefts, targets(own, lax.axis_size("mpo") // 2)):
        for place, q in enumerate(sectors):
            for w in range(terms):
                rows = pl.ds((place * terms + w) * width, width)
                copies.append(pltpu.make_async_copy(stage.at[w, q], left.at[rows], sem.at[1]))
        copies.append(pltpu.make_async_copy(wbuf, left.at[pl.ds(len(sectors) * terms * width, PAD)], sem.at[1]))
    for copy in copies:
        copy.start()
    shift = blocks.bit_length() - 1
    sources = [lax.shift_right_logical(right_sector[sec * blocks + q], shift) for q in range(blocks)]
    for q in range(blocks):
        again = jnp.bool_(False)
        for other in range(q):
            again = again | (sources[other] == sources[q])
        places[q] = sources[q] * SLOTS + jnp.where(again, 1, 0)
    for copy in copies:
        copy.wait()


def collect_left_kernel(*refs):
    *lefts, kept, given, sem = refs
    size = given.shape[1] - PAD
    copies = []
    place = 0
    for left, (_, kinds) in zip(lefts, MOVES):
        count = len(kinds)
        for j in range(count):
            for target, first in ((kept, j), (given, count + j)):
                for start, rows in ((first * size, pl.ds(0, size)), (2 * count * size, pl.ds(size, PAD))):
                    source = left.at[pl.ds(start, rows.size)]
                    copies.append(pltpu.make_async_copy(source, target.at[place, rows], sem))
            place += 1
    start_all(copies)


def collect_right_kernel(*refs):
    *rights, given, sem = refs
    copies = []
    place = 0
    for right, (_, kinds) in zip(rights, MOVES[1:]):
        count = len(kinds)
        copies.append(pltpu.make_async_copy(right.at[pl.ds(count, count)], given.at[pl.ds(place, count)], sem))
        place += count
    start_all(copies)


def order_kernel(places, arrived, *rest):
    *rights, sem = rest
    sectors = [q for group in targets(lax.axis_index("mpo"), lax.axis_size("mpo") // 2) for q in group]
    copies = []
    for right in rights:
        for place in range(right.shape[0]):
            copies.append(pltpu.make_async_copy(arrived.at[places[sectors[len(copies)]]], right.at[place], sem))
            copies[-1].start()
    for copy in copies:
        copy.wait()


def live(rows, left, right):
    row = lax.broadcasted_iota(jnp.int32, rows, 0)
    col = lax.broadcasted_iota(jnp.int32, rows, 1)
    return (row < left) & (col < right)


def total(x):
    return jnp.sum(jnp.sum(x, axis=0, keepdims=True), axis=1, keepdims=True)


def split(x):
    high = x.astype(BF16)
    return high, (x - high.astype(F32)).astype(BF16)


def apply(block, kind, lefts, rights, sides=(0, 1)):
    _, terms, width, _ = rights[sides[0]].shape
    size = terms * width
    acc = jnp.zeros((width, width), F32)
    for index, place, other in parts_of(kind):
        for side in sides:
            left = lefts[side][other, :size]
            scale = lefts[side][other, size:].astype(F32)
            if index == 0:
                right = [rights[side][place, w] for w in range(terms)]
            elif side == 0:
                right = [rights[1 + index][place, w] for w in range(terms)]
            else:
                right = [rights[-1][other - 2, w] for w in range(terms)]
            half = jnp.dot(left, block, preferred_element_type=F32)
            if block.shape[1] > width:
                half = half[:, :width] + half[:, width:]
            halves = []
            for w in range(terms):
                weight = scale[3 * w : 3 * w + 1] + scale[3 * w + 1 : 3 * w + 2] + scale[3 * w + 2 : 3 * w + 3]
                halves.append(split(weight * half[w * width : (w + 1) * width]))
            both = lax.dot_general(
                jnp.concatenate([jnp.concatenate(part, axis=1) for part in zip(*halves)], axis=0),
                jnp.concatenate(right, axis=1),
                (((1,), (1,)), ((), ())),
                preferred_element_type=F32,
            )
            acc = acc + (both[:width] + both[width:])
    return acc


def own_sector(kind):
    own = lax.axis_index("mpo")
    return sector_of(own // 2, own % 2, kind, lax.axis_size("mpo") // 2)


def start_vector(kind, left_size, right_size, right_sector, vector):
    width = vector.shape[1]
    q = own_sector(kind)
    sec = lax.axis_index("sec")
    mask = live((width, width), left_size[q], right_size[right_sector[sec * left_size.shape[0] + q]])
    return mask, jnp.where(mask, vector[kind].astype(F32), 0.0)


def load_vectors(vectors, vector, sem):
    start_all([pltpu.make_async_copy(vectors.at[own_sector(kind)], vector.at[kind], sem) for kind in range(2)])


def scaled(start):
    cells = float(start.shape[0] * start.shape[1])
    norm = total(start * start)
    unit = start * (1.0 / jnp.sqrt(norm / cells + 1e-06))
    return norm, unit, total(unit * unit)


def over(top, bottom):
    return jnp.where(bottom > 0.0, top / jnp.where(bottom > 0.0, bottom, 1.0), 0.0)


def begin_kernel(left_size, right_size, right_sector, vectors, *rest):
    *blocks, out, vector, sem = rest
    load_vectors(vectors, vector, sem)
    for kind in range(2):
        _, start = start_vector(kind, left_size, right_size, right_sector, vector)
        out[kind] = apply(start.astype(BF16), kind, blocks[:1], (blocks[1], None, *blocks[2:]), (0,))


def first_kernel(left_size, right_size, right_sector, vectors, begun, *rest):
    *blocks, out, ratios, vector, sem = rest
    load_vectors(vectors, vector, sem)
    row = lax.broadcasted_iota(jnp.int32, ratios.shape, 0)
    found = jnp.zeros(ratios.shape, F32)
    for kind in range(2):
        mask, start = start_vector(kind, left_size, right_size, right_sector, vector)
        norm, unit, length = scaled(start)
        scale = 1.0 / jnp.sqrt(norm / float(start.shape[0] * start.shape[1]) + 1e-06)
        image = begun[kind] + apply(start.astype(BF16), kind, (None, blocks[0]), (None, *blocks[1:]), (1,))
        image = jnp.where(mask, image, 0.0) * scale
        ratio = over(total(unit * image), length)
        out[kind] = (image - ratio * unit).astype(BF16)
        found = jnp.where(row == kind, ratio, found)
    ratios[...] = found


def second_kernel(left_size, right_size, right_sector, vectors, ratios, image_here, image_there, *rest):
    *blocks, out, vector, sem = rest
    width = vector.shape[1]
    upper = lax.axis_index("mpo") // 2 >= lax.axis_size("mpo") // 4
    load_vectors(vectors, vector, sem)
    parts = out.shape[0]
    rows = width // parts
    lane = lax.broadcasted_iota(jnp.int32, (8, width), 1)
    line = jnp.zeros((8, width), F32)
    rests = []
    afters = []
    for kind in range(2):
        mask, start = start_vector(kind, left_size, right_size, right_sector, vector)
        norm, unit, length = scaled(start)
        rest = image_here[kind].astype(F32) + image_there[kind].astype(F32)
        block = jnp.concatenate(split(rest), axis=1)
        after = jnp.where(mask, apply(block, kind, blocks[:2], blocks[2:]), 0.0)
        square = total(rest * rest)
        on_rest = total(rest * after)
        on_unit = total(unit * after)
        rest_ratio = over(on_rest, square)
        unit_ratio = over(on_unit, length)
        share = jnp.where(upper == (kind == 1), 1.0, 0.0)
        numbers = (
            share * norm,
            ratios[kind : kind + 1, :1],
            share * square,
            on_rest,
            on_unit,
            share * total(rest * unit),
            rest_ratio,
            unit_ratio,
        )
        after = after - rest_ratio * rest - unit_ratio * unit
        place = own_sector(kind) * LANES
        for j, number in enumerate(numbers):
            line = jnp.where(lane == place + j, number, line)
        rests.append(rest)
        afters.append(after)
    chosen = jnp.where(upper, rests[1], rests[0])
    high, _ = split(line)
    mid, low = split(line - high.astype(F32))
    row = lax.broadcasted_iota(jnp.int32, line.shape, 0)
    coded = jnp.where(row == 0, high.astype(F32), jnp.where(row == 1, mid.astype(F32), jnp.where(row == 2, low.astype(F32), 0.0)))
    for d in range(parts):
        own_rows = [x[d * rows : (d + 1) * rows] for x in (chosen, *afters)]
        out[d] = jnp.concatenate([*own_rows, coded], axis=0).astype(BF16)


def finish_kernel(left_size, right_size, right_sector, vectors, pieces, shared, next_out, rest_out, coef_out, vector, sem):
    blocks, rows, width = next_out.shape
    sec = lax.axis_index("sec")
    part = lax.axis_index("mpo")
    devices = shared.shape[0]
    groups = PAD // rows
    load = pltpu.make_async_copy(vectors.at[:, pl.ds(pl.multiple_of(part // groups * PAD, PAD), PAD)], vector, sem)
    load.start()
    entries = float(devices * blocks * width * width)
    cells = float(width * width)
    stats = shared[:, 0, :]
    line = shared[sec][:1]
    chips = lax.axis_size("mpo") // 2
    lane = lax.broadcasted_iota(jnp.int32, stats.shape, 1) % LANES

    def field(x, j):
        return x if j == 0 else pltpu.roll(x, x.shape[1] - j, 1)

    lead = lane == 0
    norm = jnp.where(lead, field(stats, 0), 0.0)
    ratio, square, on_rest, on_unit, skew = (field(stats, j) for j in range(1, 6))
    gain = 1.0 / jnp.sqrt(total(norm) / entries + 1e-06)
    mean = norm / cells + 1e-06
    weight = jnp.where(lead, (gain * gain) * mean, 0.0)
    length = norm / mean
    overlap = ratio * length + skew
    alpha = total(jnp.where(lead, weight * overlap, 0.0)) / entries
    delta = jnp.where(lead, ratio - alpha, 0.0)
    rest_total = total(jnp.where(lead, weight * (square + delta * delta * length + 2.0 * delta * skew), 0.0))
    beta = jnp.sqrt(rest_total / entries + 1e-06)
    inner = on_rest + delta * (on_unit + square + ratio * skew) + delta * delta * overlap
    alpha_next = total(jnp.where(lead, weight * inner, 0.0)) / entries / beta / beta
    for j, number in enumerate((alpha, beta, alpha_next)):
        coef_out[j] = number[0, 0]
    load.wait()
    for q in range(blocks):
        cut, kind, core = q // 4, q // 2 % 2, q % 2
        lower = 2 * ((cut + 1 + kind) % (chips // 2)) + core
        higher = lower + chips
        norm_q, ratio_q, rest_q, unit_q = (line[:, q * LANES + j : q * LANES + j + 1] for j in (0, 1, 6, 7))
        root = jnp.sqrt(norm_q / cells + 1e-06)
        scale = gain * root
        row = lax.broadcasted_iota(jnp.int32, (rows, width), 0) + part * rows
        col = lax.broadcasted_iota(jnp.int32, (rows, width), 1)
        mask = (row < left_size[q]) & (col < right_size[right_sector[sec * blocks + q]])
        group = vector[q].astype(F32)
        own_rows = group[:rows]
        for j in range(1, groups):
            own_rows = jnp.where(part % groups == j, group[j * rows : (j + 1) * rows], own_rows)
        unit = jnp.where(mask, own_rows, 0.0) / root
        sent = [pieces[owner].astype(F32) for owner in (lower, higher)]
        rest = sent[kind][:rows]
        after_rows = slice((1 + kind) * rows, (2 + kind) * rows)
        after = sent[0][after_rows] + sent[1][after_rows]
        shift = ratio_q - alpha
        second = (scale / beta) * (rest + shift * unit)
        next_out[q] = second
        on_second = rest_q + shift - alpha_next
        on_first = unit_q + shift * (ratio_q - alpha_next)
        rest_out[q] = (scale / beta) * (after + on_second * rest + on_first * unit) - (beta * scale) * unit


def shards(
    wavefunction,
    left_size,
    right_size,
    right_sector,
    left_environment,
    right_environment,
    term_weights,
):
    blocks, width, _ = wavefunction.shape
    terms = left_environment.shape[0]
    devices = lax.axis_size("sec")
    layers = lax.axis_size("mpo")
    rows = width // layers
    anywhere = pl.BlockSpec(memory_space=pl.ANY)
    scalars = pl.BlockSpec(memory_space=pltpu.SMEM)
    vmem = pl.BlockSpec(memory_space=pltpu.VMEM)

    chips = layers // 2
    long = terms * width
    routes = [[(p, (p + 2 * move) % layers) for p in range(layers)] for move, _ in MOVES]
    counts = [2 * len(kinds) for _, kinds in MOVES]
    cores = [(p, p ^ 1) for p in range(layers)]
    with jax.named_scope("pack_right"):
        right_out = pl.pallas_call(
            pack_right_kernel,
            out_shape=jax.ShapeDtypeStruct((devices, SLOTS, terms, width, width), BF16),
            in_specs=[scalars, anywhere],
            out_specs=anywhere,
            scratch_shapes=[pltpu.VMEM(right_environment.shape, BF16), pltpu.SemaphoreType.DMA((3,))],
            compiler_params=pltpu.CompilerParams(vmem_limit_bytes=60 * MIB),
        )(right_sector, right_environment)
    with jax.named_scope("right_over_sec"):
        arrived = lax.all_to_all(right_out, "sec", 0, 0, tiled=True)
    with jax.named_scope("pack_left"):
        *lefts, places = pl.pallas_call(
            pack_left_kernel,
            out_shape=[jax.ShapeDtypeStruct((count * long + PAD, width), BF16) for count in counts]
            + [jax.ShapeDtypeStruct((blocks,), jnp.int32)],
            in_specs=[scalars, scalars, anywhere],
            out_specs=[anywhere] * len(MOVES) + [scalars],
            scratch_shapes=[
                pltpu.VMEM(left_environment.shape, BF16),
                pltpu.VMEM((PAD, width), BF16),
                pltpu.SemaphoreType.DMA((2,)),
            ],
            compiler_params=pltpu.CompilerParams(vmem_limit_bytes=8 * MIB),
        )(term_weights, right_sector, left_environment)
    with jax.named_scope("left_over_z"):
        lefts = [lefts[0]] + [lax.ppermute(left, "mpo", route) for left, route in zip(lefts[1:], routes[1:])]
    with jax.named_scope("left_over_core"):
        kept, given = pl.pallas_call(
            collect_left_kernel,
            out_shape=(jax.ShapeDtypeStruct((blocks // 2, long + PAD, width), BF16),) * 2,
            in_specs=[anywhere] * len(MOVES),
            out_specs=(anywhere, anywhere),
            scratch_shapes=[pltpu.SemaphoreType.DMA],
            compiler_params=pltpu.CompilerParams(vmem_limit_bytes=4 * MIB),
        )(*lefts)
        lefts = [kept, lax.ppermute(given, "mpo", cores)]
        arrived, *lefts = lax.optimization_barrier((arrived, *lefts))
    with jax.named_scope("order"):
        rights = pl.pallas_call(
            order_kernel,
            out_shape=[jax.ShapeDtypeStruct((count, terms, width, width), BF16) for count in [2, 2] + counts[1:]],
            in_specs=[scalars, anywhere],
            out_specs=[anywhere] * (len(MOVES) + 1),
            scratch_shapes=[pltpu.SemaphoreType.DMA],
            compiler_params=pltpu.CompilerParams(vmem_limit_bytes=4 * MIB),
        )(places, arrived.reshape(devices * SLOTS, terms, width, width))
    with jax.named_scope("right_over_z"):
        stayed = [rights[0], lax.ppermute(rights[1], "mpo", cores)]
        rights = [lax.ppermute(right, "mpo", route) for right, route in zip(rights[2:], routes[1:])]
    with jax.named_scope("right_over_core"):
        given = pl.pallas_call(
            collect_right_kernel,
            out_shape=jax.ShapeDtypeStruct((blocks // 2 - 2, terms, width, width), BF16),
            in_specs=[anywhere] * (len(MOVES) - 1),
            out_specs=anywhere,
            scratch_shapes=[pltpu.SemaphoreType.DMA],
            compiler_params=pltpu.CompilerParams(vmem_limit_bytes=4 * MIB),
        )(*rights)
        rights = stayed + rights + [lax.ppermute(given, "mpo", cores)]
    with jax.named_scope("first_image"):
        begun = pl.pallas_call(
            begin_kernel,
            out_shape=jax.ShapeDtypeStruct((2, width, width), F32),
            in_specs=[scalars, scalars, scalars, anywhere] + [vmem] * (len(MOVES) + 1),
            out_specs=vmem,
            scratch_shapes=[pltpu.VMEM((2, width, width), BF16), pltpu.SemaphoreType.DMA],
            compiler_params=pltpu.CompilerParams(vmem_limit_bytes=16 * MIB),
            cost_estimate=pl.CostEstimate(flops=6 * width**3 * blocks, bytes_accessed=MIB, transcendentals=0),
        )(left_size, right_size, right_sector, wavefunction, lefts[0], rights[0], *rights[2:-1])
        image_here, ratios = pl.pallas_call(
            first_kernel,
            out_shape=(
                jax.ShapeDtypeStruct((2, width, width), BF16),
                jax.ShapeDtypeStruct((8, width), F32),
            ),
            in_specs=[scalars, scalars, scalars, anywhere] + [vmem] * 4,
            out_specs=(vmem, vmem),
            scratch_shapes=[pltpu.VMEM((2, width, width), BF16), pltpu.SemaphoreType.DMA],
            compiler_params=pltpu.CompilerParams(vmem_limit_bytes=16 * MIB),
        )(left_size, right_size, right_sector, wavefunction, begun, lefts[1], rights[1], rights[-1])
    with jax.named_scope("swap_images"):
        image_there = lax.ppermute(image_here, "mpo", [(p, (p + chips) % layers) for p in range(layers)])
    with jax.named_scope("second_image"):
        pieces = pl.pallas_call(
            second_kernel,
            out_shape=jax.ShapeDtypeStruct((layers, 3 * rows + 8, width), BF16),
            in_specs=[scalars, scalars, scalars, anywhere] + [vmem] * (len(MOVES) + 7),
            out_specs=vmem,
            scratch_shapes=[pltpu.VMEM((2, width, width), BF16), pltpu.SemaphoreType.DMA],
            compiler_params=pltpu.CompilerParams(vmem_limit_bytes=16 * MIB),
        )(left_size, right_size, right_sector, wavefunction, ratios, image_here, image_there, *lefts, *rights)
    with jax.named_scope("rows_over_mpo"):
        pieces = lax.all_to_all(pieces, "mpo", 0, 0, tiled=True)
    with jax.named_scope("numbers_over_sec"):
        line = jnp.sum(pieces[:, 3 * rows :, :].astype(F32), axis=(0, 1))
        shared = lax.all_to_all(jnp.broadcast_to(line[None, None], (devices, 8, width)), "sec", 0, 0, tiled=True)
    with jax.named_scope("finish"):
        next_vector, residual, coefficients = pl.pallas_call(
            finish_kernel,
            out_shape=(
                jax.ShapeDtypeStruct((blocks, rows, width), F32),
                jax.ShapeDtypeStruct((blocks, rows, width), F32),
                jax.ShapeDtypeStruct((3,), F32),
            ),
            in_specs=[scalars, scalars, scalars, anywhere, vmem, vmem],
            out_specs=(vmem, vmem, scalars),
            scratch_shapes=[pltpu.VMEM((blocks, PAD, width), BF16), pltpu.SemaphoreType.DMA],
            compiler_params=pltpu.CompilerParams(vmem_limit_bytes=8 * MIB),
        )(left_size, right_size, right_sector, wavefunction, pieces, shared)
    return (next_vector, residual, coefficients)


def solution(mesh):
    placed = (
        P("sec", None, None),
        P("sec"),
        P(),
        P(),
        P("mpo", "sec", None, None),
        P("mpo", "sec", None, None),
        P("mpo"),
    )
    return jax.shard_map(
        shards,
        mesh=mesh,
        in_specs=placed,
        out_specs=(P("sec", "mpo", None), P("sec", "mpo", None), P()),
        check_vma=False,
    )
```

```python
import jax
import jax.numpy as jnp
from jax import lax
from jax.experimental import pallas as pl
from jax.experimental.pallas import tpu as pltpu
from jax.sharding import PartitionSpec as P

F32 = jnp.float32
BF16 = jnp.bfloat16
SLOTS = 2
PAD = 16
LANES = 8
MIB = 1024 * 1024


def sector_of(chip, core, kind, chips):
    cuts = chips // 2
    return ((chip + chips - 1 - kind) % cuts) * 4 + kind * 2 + core


MOVES = ((0, (0, 1)), (2, (1,)), (-2, (0,)), (1, (0, 1)), (-1, (0, 1)))


def targets(own, chips):
    chip, core = own // 2, own % 2
    return [
        [sector_of((chip + move + chips) % chips, (core + side) % 2, kind, chips) for side in range(2) for kind in kinds]
        for move, kinds in MOVES
    ]


def parts_of(kind):
    found = []
    base = 0
    for index, (_, kinds) in enumerate(MOVES):
        if kind in kinds:
            found.append((index, kinds.index(kind), base + kinds.index(kind)))
        base += len(kinds)
    return found


def start_all(copies):
    for copy in copies:
        copy.start()
    for copy in copies:
        copy.wait()


def pack_right_kernel(right_sector, right_env, right_out, stage, sem):
    blocks = right_env.shape[1]
    devices = right_out.shape[0]
    sec = lax.axis_index("sec")
    load = pltpu.make_async_copy(right_env, stage, sem.at[0])
    load.start()
    base = sec * blocks
    picks = []
    copies = []
    seconds = []
    for t in range(devices):
        first = jnp.int32(blocks * blocks)
        last = jnp.int32(0)
        for i in range(blocks):
            offset = right_sector[t * blocks + i] - base
            match = (offset >= 0) & (offset < blocks)
            first = jnp.where(match, jnp.minimum(first, offset + i * blocks), first)
            last = jnp.where(match, offset, last)
        picks.append((first & (blocks - 1), last))
        if t < devices // 4:
            continue
        if t == devices // 4:
            load.wait()
        for ready in range(t + 1 if t == devices // 4 else 1):
            target = ready if t == devices // 4 else t
            first, last = picks[target]
            copy = pltpu.make_async_copy(stage.at[:, first], right_out.at[target, 0], sem.at[1])
            copy.start()
            copies.append(copy)
            copy = pltpu.make_async_copy(stage.at[:, last], right_out.at[target, 1], sem.at[2])
            pl.when(first != last)(copy.start)
            seconds.append((first != last, copy))
    for copy in copies:
        copy.wait()
    for there, copy in seconds:
        pl.when(there)(copy.wait)


def pack_left_kernel(weights, right_sector, left_env, *rest):
    *lefts, places, stage, wbuf, sem = rest
    terms, blocks, width, _ = left_env.shape
    sec = lax.axis_index("sec")
    own = lax.axis_index("mpo")
    load = pltpu.make_async_copy(left_env, stage, sem.at[0])
    load.start()
    row = lax.broadcasted_iota(jnp.int32, wbuf.shape, 0)
    vals = jnp.zeros(wbuf.shape, F32)
    for w in range(terms):
        whole = jnp.full(wbuf.shape, weights[w], F32)
        high = whole.astype(BF16).astype(F32)
        mid = (whole - high).astype(BF16).astype(F32)
        low = whole - high - mid
        for j, part in enumerate((high, mid, low)):
            vals = jnp.where(row == w * 3 + j, part, vals)
    wbuf[...] = vals.astype(BF16)
    load.wait()
    copies = []
    for left, sectors in zip(lefts, targets(own, lax.axis_size("mpo") // 2)):
        for place, q in enumerate(sectors):
            for w in range(terms):
                rows = pl.ds((place * terms + w) * width, width)
                copies.append(pltpu.make_async_copy(stage.at[w, q], left.at[rows], sem.at[1]))
        copies.append(pltpu.make_async_copy(wbuf, left.at[pl.ds(len(sectors) * terms * width, PAD)], sem.at[1]))
    for copy in copies:
        copy.start()
    shift = blocks.bit_length() - 1
    sources = [lax.shift_right_logical(right_sector[sec * blocks + q], shift) for q in range(blocks)]
    for q in range(blocks):
        again = jnp.bool_(False)
        for other in range(q):
            again = again | (sources[other] == sources[q])
        places[q] = sources[q] * SLOTS + jnp.where(again, 1, 0)
    for copy in copies:
        copy.wait()


def collect_left_kernel(*refs):
    *lefts, kept, given, sem = refs
    size = given.shape[1] - PAD
    copies = []
    place = 0
    for left, (_, kinds) in zip(lefts, MOVES):
        count = len(kinds)
        for j in range(count):
            for target, first in ((kept, j), (given, count + j)):
                for start, rows in ((first * size, pl.ds(0, size)), (2 * count * size, pl.ds(size, PAD))):
                    source = left.at[pl.ds(start, rows.size)]
                    copies.append(pltpu.make_async_copy(source, target.at[place, rows], sem))
            place += 1
    start_all(copies)


def collect_right_kernel(*refs):
    *rights, given, sem = refs
    copies = []
    place = 0
    for right, (_, kinds) in zip(rights, MOVES[1:]):
        count = len(kinds)
        copies.append(pltpu.make_async_copy(right.at[pl.ds(count, count)], given.at[pl.ds(place, count)], sem))
        place += count
    start_all(copies)


def order_kernel(places, arrived, *rest):
    *rights, sem = rest
    sectors = [q for group in targets(lax.axis_index("mpo"), lax.axis_size("mpo") // 2) for q in group]
    copies = []
    for right in rights:
        for place in range(right.shape[0]):
            copies.append(pltpu.make_async_copy(arrived.at[places[sectors[len(copies)]]], right.at[place], sem))
            copies[-1].start()
    for copy in copies:
        copy.wait()


def live(rows, left, right):
    row = lax.broadcasted_iota(jnp.int32, rows, 0)
    col = lax.broadcasted_iota(jnp.int32, rows, 1)
    return (row < left) & (col < right)


def total(x):
    return jnp.sum(jnp.sum(x, axis=0, keepdims=True), axis=1, keepdims=True)


def split(x):
    high = x.astype(BF16)
    return high, (x - high.astype(F32)).astype(BF16)


def apply(block, kind, lefts, rights, sides=(0, 1)):
    _, terms, width, _ = rights[sides[0]].shape
    size = terms * width
    acc = jnp.zeros((width, width), F32)
    for index, place, other in parts_of(kind):
        for side in sides:
            left = lefts[side][other, :size]
            scale = lefts[side][other, size:].astype(F32)
            if index == 0:
                right = [rights[side][place, w] for w in range(terms)]
            elif side == 0:
                right = [rights[1 + index][place, w] for w in range(terms)]
            else:
                right = [rights[-1][other - 2, w] for w in range(terms)]
            half = jnp.dot(left, block, preferred_element_type=F32)
            if block.shape[1] > width:
                half = half[:, :width] + half[:, width:]
            halves = []
            for w in range(terms):
                weight = scale[3 * w : 3 * w + 1] + scale[3 * w + 1 : 3 * w + 2] + scale[3 * w + 2 : 3 * w + 3]
                halves.append(split(weight * half[w * width : (w + 1) * width]))
            both = lax.dot_general(
                jnp.concatenate([jnp.concatenate(part, axis=1) for part in zip(*halves)], axis=0),
                jnp.concatenate(right, axis=1),
                (((1,), (1,)), ((), ())),
                preferred_element_type=F32,
            )
            acc = acc + (both[:width] + both[width:])
    return acc


def own_sector(kind):
    own = lax.axis_index("mpo")
    return sector_of(own // 2, own % 2, kind, lax.axis_size("mpo") // 2)


def start_vector(kind, left_size, right_size, right_sector, vector):
    width = vector.shape[1]
    q = own_sector(kind)
    sec = lax.axis_index("sec")
    mask = live((width, width), left_size[q], right_size[right_sector[sec * left_size.shape[0] + q]])
    return mask, jnp.where(mask, vector[kind].astype(F32), 0.0)


def load_vectors(vectors, vector, sem):
    start_all([pltpu.make_async_copy(vectors.at[own_sector(kind)], vector.at[kind], sem) for kind in range(2)])


def scaled(start):
    cells = float(start.shape[0] * start.shape[1])
    norm = total(start * start)
    unit = start * (1.0 / jnp.sqrt(norm / cells + 1e-06))
    return norm, unit, total(unit * unit)


def over(top, bottom):
    return jnp.where(bottom > 0.0, top / jnp.where(bottom > 0.0, bottom, 1.0), 0.0)


def begin_kernel(left_size, right_size, right_sector, vectors, *rest):
    *blocks, out, vector, sem = rest
    load_vectors(vectors, vector, sem)
    for kind in range(2):
        _, start = start_vector(kind, left_size, right_size, right_sector, vector)
        out[kind] = apply(start.astype(BF16), kind, blocks[:1], (blocks[1], None, *blocks[2:]), (0,))


def first_kernel(left_size, right_size, right_sector, vectors, begun, *rest):
    *blocks, out, ratios, vector, sem = rest
    load_vectors(vectors, vector, sem)
    row = lax.broadcasted_iota(jnp.int32, ratios.shape, 0)
    found = jnp.zeros(ratios.shape, F32)
    for kind in range(2):
        mask, start = start_vector(kind, left_size, right_size, right_sector, vector)
        norm, unit, length = scaled(start)
        scale = 1.0 / jnp.sqrt(norm / float(start.shape[0] * start.shape[1]) + 1e-06)
        image = begun[kind] + apply(start.astype(BF16), kind, (None, blocks[0]), (None, *blocks[1:]), (1,))
        image = jnp.where(mask, image, 0.0) * scale
        ratio = over(total(unit * image), length)
        out[kind] = (image - ratio * unit).astype(BF16)
        found = jnp.where(row == kind, ratio, found)
    ratios[...] = found


def second_kernel(left_size, right_size, right_sector, vectors, ratios, image_here, image_there, *rest):
    *blocks, out, vector, sem = rest
    width = vector.shape[1]
    upper = lax.axis_index("mpo") // 2 >= lax.axis_size("mpo") // 4
    load_vectors(vectors, vector, sem)
    parts = out.shape[0]
    rows = width // parts
    lane = lax.broadcasted_iota(jnp.int32, (8, width), 1)
    line = jnp.zeros((8, width), F32)
    rests = []
    afters = []
    for kind in range(2):
        mask, start = start_vector(kind, left_size, right_size, right_sector, vector)
        norm, unit, length = scaled(start)
        rest = image_here[kind].astype(F32) + image_there[kind].astype(F32)
        block = jnp.concatenate(split(rest), axis=1)
        after = jnp.where(mask, apply(block, kind, blocks[:2], blocks[2:]), 0.0)
        square = total(rest * rest)
        on_rest = total(rest * after)
        on_unit = total(unit * after)
        rest_ratio = over(on_rest, square)
        unit_ratio = over(on_unit, length)
        share = jnp.where(upper == (kind == 1), 1.0, 0.0)
        numbers = (
            share * norm,
            ratios[kind : kind + 1, :1],
            share * square,
            on_rest,
            on_unit,
            share * total(rest * unit),
            rest_ratio,
            unit_ratio,
        )
        after = after - rest_ratio * rest - unit_ratio * unit
        place = own_sector(kind) * LANES
        for j, number in enumerate(numbers):
            line = jnp.where(lane == place + j, number, line)
        rests.append(rest)
        afters.append(after)
    chosen = jnp.where(upper, rests[1], rests[0])
    high, _ = split(line)
    mid, low = split(line - high.astype(F32))
    row = lax.broadcasted_iota(jnp.int32, line.shape, 0)
    coded = jnp.where(row == 0, high.astype(F32), jnp.where(row == 1, mid.astype(F32), jnp.where(row == 2, low.astype(F32), 0.0)))
    for d in range(parts):
        own_rows = [x[d * rows : (d + 1) * rows] for x in (chosen, *afters)]
        out[d] = jnp.concatenate([*own_rows, coded], axis=0).astype(BF16)


def finish_kernel(left_size, right_size, right_sector, vectors, pieces, shared, next_out, rest_out, coef_out, vector, sem):
    blocks, rows, width = next_out.shape
    sec = lax.axis_index("sec")
    part = lax.axis_index("mpo")
    devices = shared.shape[0]
    groups = PAD // rows
    load = pltpu.make_async_copy(vectors.at[:, pl.ds(pl.multiple_of(part // groups * PAD, PAD), PAD)], vector, sem)
    load.start()
    entries = float(devices * blocks * width * width)
    cells = float(width * width)
    stats = shared[:, 0, :]
    line = shared[sec][:1]
    chips = lax.axis_size("mpo") // 2
    lane = lax.broadcasted_iota(jnp.int32, stats.shape, 1) % LANES

    def field(x, j):
        return x if j == 0 else pltpu.roll(x, x.shape[1] - j, 1)

    lead = lane == 0
    norm = jnp.where(lead, field(stats, 0), 0.0)
    ratio, square, on_rest, on_unit, skew = (field(stats, j) for j in range(1, 6))
    mean = norm / cells + 1e-06
    gain = 1.0 / jnp.sqrt(total(norm) / entries + 1e-06)
    weight = jnp.where(lead, (gain * gain) * mean, 0.0)
    length = norm / mean
    overlap = ratio * length + skew
    alpha = total(jnp.where(lead, weight * overlap, 0.0)) / entries
    delta = jnp.where(lead, ratio - alpha, 0.0)
    rest_total = total(jnp.where(lead, weight * (square + delta * delta * length + 2.0 * delta * skew), 0.0))
    beta = jnp.sqrt(rest_total / entries + 1e-06)
    inner = on_rest + delta * (on_unit + square + ratio * skew) + delta * delta * overlap
    alpha_next = total(jnp.where(lead, weight * inner, 0.0)) / entries / beta / beta
    for j, number in enumerate((alpha, beta, alpha_next)):
        coef_out[j] = number[0, 0]
    load.wait()
    for q in range(blocks):
        cut, kind, core = q // 4, q // 2 % 2, q % 2
        lower = 2 * ((cut + 1 + kind) % (chips // 2)) + core
        higher = lower + chips
        norm_q, ratio_q, rest_q, unit_q = (line[:, q * LANES + j : q * LANES + j + 1] for j in (0, 1, 6, 7))
        root = jnp.sqrt(norm_q / cells + 1e-06)
        scale = gain * root
        row = lax.broadcasted_iota(jnp.int32, (rows, width), 0) + part * rows
        col = lax.broadcasted_iota(jnp.int32, (rows, width), 1)
        mask = (row < left_size[q]) & (col < right_size[right_sector[sec * blocks + q]])
        group = vector[q].astype(F32)
        own_rows = group[:rows]
        for j in range(1, groups):
            own_rows = jnp.where(part % groups == j, group[j * rows : (j + 1) * rows], own_rows)
        unit = jnp.where(mask, own_rows, 0.0) * (1.0 / root)
        sent = [pieces[owner].astype(F32) for owner in (lower, higher)]
        rest = sent[kind][:rows]
        after_rows = slice((1 + kind) * rows, (2 + kind) * rows)
        after = sent[0][after_rows] + sent[1][after_rows]
        shift = ratio_q - alpha
        second = (scale / beta) * (rest + shift * unit)
        next_out[q] = second
        on_second = rest_q + shift - alpha_next
        on_first = unit_q + shift * (ratio_q - alpha_next)
        rest_out[q] = (scale / beta) * (after + on_second * rest + on_first * unit) - (beta * scale) * unit


def shards(
    wavefunction,
    left_size,
    right_size,
    right_sector,
    left_environment,
    right_environment,
    term_weights,
):
    blocks, width, _ = wavefunction.shape
    terms = left_environment.shape[0]
    devices = lax.axis_size("sec")
    layers = lax.axis_size("mpo")
    rows = width // layers
    anywhere = pl.BlockSpec(memory_space=pl.ANY)
    scalars = pl.BlockSpec(memory_space=pltpu.SMEM)
    vmem = pl.BlockSpec(memory_space=pltpu.VMEM)

    chips = layers // 2
    long = terms * width
    routes = [[(p, (p + 2 * move) % layers) for p in range(layers)] for move, _ in MOVES]
    counts = [2 * len(kinds) for _, kinds in MOVES]
    cores = [(p, p ^ 1) for p in range(layers)]
    with jax.named_scope("pack_right"):
        right_out = pl.pallas_call(
            pack_right_kernel,
            out_shape=jax.ShapeDtypeStruct((devices, SLOTS, terms, width, width), BF16),
            in_specs=[scalars, anywhere],
            out_specs=anywhere,
            scratch_shapes=[pltpu.VMEM(right_environment.shape, BF16), pltpu.SemaphoreType.DMA((3,))],
            compiler_params=pltpu.CompilerParams(vmem_limit_bytes=60 * MIB),
        )(right_sector, right_environment)
    with jax.named_scope("right_over_sec"):
        arrived = lax.all_to_all(right_out, "sec", 0, 0, tiled=True)
    with jax.named_scope("pack_left"):
        *lefts, places = pl.pallas_call(
            pack_left_kernel,
            out_shape=[jax.ShapeDtypeStruct((count * long + PAD, width), BF16) for count in counts]
            + [jax.ShapeDtypeStruct((blocks,), jnp.int32)],
            in_specs=[scalars, scalars, anywhere],
            out_specs=[anywhere] * len(MOVES) + [scalars],
            scratch_shapes=[
                pltpu.VMEM(left_environment.shape, BF16),
                pltpu.VMEM((PAD, width), BF16),
                pltpu.SemaphoreType.DMA((2,)),
            ],
            compiler_params=pltpu.CompilerParams(vmem_limit_bytes=8 * MIB),
        )(term_weights, right_sector, left_environment)
    with jax.named_scope("left_over_z"):
        lefts = [lefts[0]] + [lax.ppermute(left, "mpo", route) for left, route in zip(lefts[1:], routes[1:])]
    with jax.named_scope("left_over_core"):
        kept, given = pl.pallas_call(
            collect_left_kernel,
            out_shape=(jax.ShapeDtypeStruct((blocks // 2, long + PAD, width), BF16),) * 2,
            in_specs=[anywhere] * len(MOVES),
            out_specs=(anywhere, anywhere),
            scratch_shapes=[pltpu.SemaphoreType.DMA],
            compiler_params=pltpu.CompilerParams(vmem_limit_bytes=4 * MIB),
        )(*lefts)
        lefts = [kept, lax.ppermute(given, "mpo", cores)]
        arrived, *lefts = lax.optimization_barrier((arrived, *lefts))
    with jax.named_scope("order"):
        rights = pl.pallas_call(
            order_kernel,
            out_shape=[jax.ShapeDtypeStruct((count, terms, width, width), BF16) for count in [2, 2] + counts[1:]],
            in_specs=[scalars, anywhere],
            out_specs=[anywhere] * (len(MOVES) + 1),
            scratch_shapes=[pltpu.SemaphoreType.DMA],
            compiler_params=pltpu.CompilerParams(vmem_limit_bytes=4 * MIB),
        )(places, arrived.reshape(devices * SLOTS, terms, width, width))
    with jax.named_scope("right_over_z"):
        stayed = [rights[0], lax.ppermute(rights[1], "mpo", cores)]
        rights = [lax.ppermute(right, "mpo", route) for right, route in zip(rights[2:], routes[1:])]
    with jax.named_scope("right_over_core"):
        given = pl.pallas_call(
            collect_right_kernel,
            out_shape=jax.ShapeDtypeStruct((blocks // 2 - 2, terms, width, width), BF16),
            in_specs=[anywhere] * (len(MOVES) - 1),
            out_specs=anywhere,
            scratch_shapes=[pltpu.SemaphoreType.DMA],
            compiler_params=pltpu.CompilerParams(vmem_limit_bytes=4 * MIB),
        )(*rights)
        rights = stayed + rights + [lax.ppermute(given, "mpo", cores)]
    with jax.named_scope("first_image"):
        begun = pl.pallas_call(
            begin_kernel,
            out_shape=jax.ShapeDtypeStruct((2, width, width), F32),
            in_specs=[scalars, scalars, scalars, anywhere] + [vmem] * (len(MOVES) + 1),
            out_specs=vmem,
            scratch_shapes=[pltpu.VMEM((2, width, width), BF16), pltpu.SemaphoreType.DMA],
            compiler_params=pltpu.CompilerParams(vmem_limit_bytes=16 * MIB),
            cost_estimate=pl.CostEstimate(flops=6 * width**3 * blocks, bytes_accessed=MIB, transcendentals=0),
        )(left_size, right_size, right_sector, wavefunction, lefts[0], rights[0], *rights[2:-1])
        image_here, ratios = pl.pallas_call(
            first_kernel,
            out_shape=(
                jax.ShapeDtypeStruct((2, width, width), BF16),
                jax.ShapeDtypeStruct((8, width), F32),
            ),
            in_specs=[scalars, scalars, scalars, anywhere] + [vmem] * 4,
            out_specs=(vmem, vmem),
            scratch_shapes=[pltpu.VMEM((2, width, width), BF16), pltpu.SemaphoreType.DMA],
            compiler_params=pltpu.CompilerParams(vmem_limit_bytes=16 * MIB),
        )(left_size, right_size, right_sector, wavefunction, begun, lefts[1], rights[1], rights[-1])
    with jax.named_scope("swap_images"):
        image_there = lax.ppermute(image_here, "mpo", [(p, (p + chips) % layers) for p in range(layers)])
    with jax.named_scope("second_image"):
        pieces = pl.pallas_call(
            second_kernel,
            out_shape=jax.ShapeDtypeStruct((layers, 3 * rows + 8, width), BF16),
            in_specs=[scalars, scalars, scalars, anywhere] + [vmem] * (len(MOVES) + 7),
            out_specs=vmem,
            scratch_shapes=[pltpu.VMEM((2, width, width), BF16), pltpu.SemaphoreType.DMA],
            compiler_params=pltpu.CompilerParams(vmem_limit_bytes=16 * MIB),
        )(left_size, right_size, right_sector, wavefunction, ratios, image_here, image_there, *lefts, *rights)
    with jax.named_scope("rows_over_mpo"):
        pieces = lax.all_to_all(pieces, "mpo", 0, 0, tiled=True)
    with jax.named_scope("numbers_over_sec"):
        line = jnp.sum(pieces[:, 3 * rows :, :].astype(F32), axis=(0, 1))
        shared = lax.all_to_all(jnp.broadcast_to(line[None, None], (devices, 8, width)), "sec", 0, 0, tiled=True)
    with jax.named_scope("finish"):
        next_vector, residual, coefficients = pl.pallas_call(
            finish_kernel,
            out_shape=(
                jax.ShapeDtypeStruct((blocks, rows, width), F32),
                jax.ShapeDtypeStruct((blocks, rows, width), F32),
                jax.ShapeDtypeStruct((3,), F32),
            ),
            in_specs=[scalars, scalars, scalars, anywhere, vmem, vmem],
            out_specs=(vmem, vmem, scalars),
            scratch_shapes=[pltpu.VMEM((blocks, PAD, width), BF16), pltpu.SemaphoreType.DMA],
            compiler_params=pltpu.CompilerParams(vmem_limit_bytes=8 * MIB),
        )(left_size, right_size, right_sector, wavefunction, pieces, shared)
    return (next_vector, residual, coefficients)


def solution(mesh):
    placed = (
        P("sec", None, None),
        P("sec"),
        P(),
        P(),
        P("mpo", "sec", None, None),
        P("mpo", "sec", None, None),
        P("mpo"),
    )
    return jax.shard_map(
        shards,
        mesh=mesh,
        in_specs=placed,
        out_specs=(P("sec", "mpo", None), P("sec", "mpo", None), P()),
        check_vma=False,
    )
```
